128 devices in a mesh: engine: 4 (over y), tp: 32 (over x, z, core).
Axes of the slice: x: 4, y: 4, z: 4, core: 2. Of those that a mesh axis runs over, the one named last changes fastest.
Arguments:
- trainer_panels: bfloat16 [256, 64, 18432], P(('engine', 'tp')), may hold values from -1 to 1
- panel_ids: int32 [256], P(('engine', 'tp')), may hold values from 0 to 128, as said below
- first_tokens: bfloat16 [512, 8192], P('engine'), may hold values from -6 to 6
- second_tokens: bfloat16 [512, 8192], P('engine'), may hold values from -6 to 6
- norm_gain: float32 [8192], replicated, may hold values from 0.5 to 1.5
- kv_cache: bfloat16 [4, 768, 128, 2048], P('engine', 'tp'), may hold values from -6 to 6
- block_table: int32 [512, 6], P(('engine', 'tp')), may hold values from 0 to 23, as said below
- lengths: int32 [512], P(('engine', 'tp')), may hold values from 4 to 766
- move_list: int32 [4, 32, 4, 1], P('engine', 'tp'), may hold values from 0 to 24, as said below
Outputs:
- first_out: bfloat16 [512, 8192], P('engine', 'tp')
- second_out: bfloat16 [512, 8192], P('engine', 'tp')
- hosted: bfloat16 [4, 128, 128, 2048], P('engine', 'tp')
The draws below stay inside these ranges and needn't reach their ends.
Inputs may be any that keep to these rules, and one draw needn't show every extreme that they name: `panel_ids`: every panel 0 to 127 stands in exactly one slot; the other slots hold 128; the slots of some device are all full. `block_table`: the entries of one device's rollouts list each of its 24 blocks once. `move_list`: A device never names a block for its own engine, and names each block at most once.
All inputs are finite; a program needn't handle non-finite values.
Results may differ from the reference program's by a relative error of at most 0.02.
Values may be sent and summed in bfloat16 or wider, within the bound.
No kernel may reach another device: no remote copies, remote signals or barrier semaphores. Data moves between devices by JAX's collectives and lax.ppermute only.
A program may use at most 256 MiB of HBM per device.

```python
import math
import jax
import jax.numpy as jnp
from jax import lax

D = 8192
HEADS = 64
KVH = 8
HD = 128
PANELS = 128
BLK = 128
MAXB = 6
MSLOT = 1
ROLLOUTS = 512
R_DEV = 4
NBLK = 24
CAP = 2
PR = 64
COLS = 18432
N_ENGINE = 4
N_TP = 32


def draw_trainer_panels(key, part):
    key = jax.random.fold_in(key, 61)
    slots = N_ENGINE * N_TP * CAP
    key_a = jax.random.fold_in(key, 0)
    result = jnp.clip(jax.random.normal(key_a, (slots, PR, COLS), jnp.float32), -6.0, 6.0) * D ** (-0.5)
    return result.astype(jnp.bfloat16)


def draw_first_tokens(key, part):
    key = jax.random.fold_in(key, 71)
    key_a = jax.random.fold_in(key, 0)
    noise = jax.random.normal(key_a, (ROLLOUTS, D), jnp.float32)
    result = jnp.clip(noise, -6.0, 6.0)
    return result.astype(jnp.bfloat16)


def draw_second_tokens(key, part):
    key = jax.random.fold_in(key, 79)
    key_a = jax.random.fold_in(key, 0)
    noise = jax.random.normal(key_a, (ROLLOUTS, D), jnp.float32)
    result = jnp.clip(noise, -6.0, 6.0)
    return result.astype(jnp.bfloat16)


def draw_kv_cache(key, part):
    key = jax.random.fold_in(key, 83)
    width = 2 * KVH * HD
    shape = (N_ENGINE, N_TP * NBLK, BLK, width)
    result = jnp.clip(jax.random.normal(key, shape, jnp.float32), -6.0, 6.0)
    return result.astype(jnp.bfloat16)


def draw_panel_ids(key, part):
    key = jax.random.fold_in(key, 11)
    slots = N_ENGINE * N_TP * CAP
    key_a, key_b = jax.random.split(key)
    rest = jax.random.permutation(key_a, slots - CAP) + CAP
    base = jnp.concatenate([jnp.arange(CAP, dtype=jnp.int32), rest.astype(jnp.int32)])
    shift = jax.random.randint(key_b, (), 0, N_ENGINE * N_TP) * CAP
    base = jnp.roll(base, shift)
    return jnp.where(base < PANELS, base, PANELS).astype(jnp.int32)


def draw_block_table(key, part):
    key = jax.random.fold_in(key, 23)
    groups = ROLLOUTS // R_DEV
    nblk = R_DEV * MAXB
    keys = jax.random.split(key, groups)
    perms = jax.vmap(lambda k: jax.random.permutation(k, nblk))(keys)
    return perms.reshape(ROLLOUTS, MAXB).astype(jnp.int32)


def draw_lengths(key, part):
    key = jax.random.fold_in(key, 37)
    top = MAXB * BLK - 2
    key_a, key_b, key_c, key_d = jax.random.split(key, 4)
    short = jax.random.randint(key_a, (ROLLOUTS,), 4, max(top // 4, 4) + 1)
    longer = jax.random.randint(key_b, (ROLLOUTS,), top // 4 + 1, top + 1)
    pick = jax.random.randint(key_c, (ROLLOUTS,), 0, 8) == 0
    result = jnp.where(pick, longer, short)
    peak = jax.random.randint(key_d, (), 0, ROLLOUTS)
    return result.at[peak].set(top).astype(jnp.int32)


def draw_move_list(key, part):
    key = jax.random.fold_in(key, 53)
    nblk = R_DEV * MAXB
    key_a, key_b = jax.random.split(key)
    keys = jax.random.split(key_a, N_ENGINE * N_TP)
    perms = jax.vmap(lambda k: jax.random.permutation(k, nblk))(keys)
    chosen = perms[:, :N_ENGINE * MSLOT].reshape(N_ENGINE, N_TP, N_ENGINE, MSLOT)
    used = jax.random.randint(key_b, (N_ENGINE, N_TP, N_ENGINE, MSLOT), 0, 3) != 0
    source = jnp.arange(N_ENGINE, dtype=jnp.int32)[:, None, None, None]
    target = jnp.arange(N_ENGINE, dtype=jnp.int32)[None, None, :, None]
    keep = jnp.logical_and(used, source != target)
    return jnp.where(keep, chosen, nblk).astype(jnp.int32)


def setup_inputs(seed: int = 0) -> dict:
    key_list = jax.random.split(jax.random.key(seed), 10)
    return {
        "trainer_panels": draw_trainer_panels(jax.random.fold_in(key_list[9], 71), 0),
        "panel_ids": draw_panel_ids(jax.random.fold_in(key_list[9], 71), 0),
        "first_tokens": draw_first_tokens(jax.random.fold_in(key_list[9], 71), 0),
        "second_tokens": draw_second_tokens(jax.random.fold_in(key_list[9], 71), 0),
        "norm_gain": jnp.clip(1.0 + 0.1 * jax.random.normal(key_list[4], (D,), jnp.float32), 0.5, 1.5),
        "kv_cache": draw_kv_cache(jax.random.fold_in(key_list[9], 71), 0),
        "block_table": draw_block_table(jax.random.fold_in(key_list[9], 71), 0),
        "lengths": draw_lengths(jax.random.fold_in(key_list[9], 71), 0),
        "move_list": draw_move_list(jax.random.fold_in(key_list[9], 71), 0),
    }


def assemble(trainer_panels, panel_ids):
    slots = trainer_panels.shape[0]
    match = panel_ids[None, :] == jnp.arange(PANELS, dtype=jnp.int32)[:, None]
    slot_of = lax.optimization_barrier(jnp.sum(jnp.where(match, jnp.arange(slots, dtype=jnp.int32)[None, :], 0), axis=1)).astype(jnp.int32)
    return jnp.take(trainer_panels, slot_of, axis=0).reshape(D, COLS)

def attend(query, cache, table, limit):
    groups = ROLLOUTS // R_DEV
    span = MAXB * BLK

    def one_group(items):
        group_query, group_table, group_limit = items
        blocks = jnp.take(cache, group_table, axis=0).reshape(R_DEV, span, KVH, 2 * HD)
        keys = blocks[..., :HD].astype(jnp.float32)
        values = blocks[..., HD:].astype(jnp.float32)
        heads = group_query.reshape(R_DEV, KVH, HEADS // KVH, HD).astype(jnp.float32)
        scores = jnp.einsum('rgjd,rlgd->rgjl', heads, keys) / math.sqrt(HD)
        visible = jnp.arange(span, dtype=jnp.int32)[None, :] < group_limit[:, None]
        scores = jnp.where(visible[:, None, None, :], scores, -1e+30)
        probs = jax.nn.softmax(scores, axis=-1).astype(jnp.bfloat16)
        mixed = jnp.einsum('rgjl,rlgd->rgjd', probs.astype(jnp.float32), values)
        return mixed.astype(jnp.bfloat16).reshape(R_DEV, HEADS * HD)
    result = lax.map(one_group, (query.reshape(groups, R_DEV, HEADS * HD), table.reshape(groups, R_DEV, MAXB), limit.reshape(groups, R_DEV)))
    return result.reshape(ROLLOUTS, HEADS * HD)

def project(mixed, w_ot):
    group = D // N_TP

    def add_group(total, index):
        part_in = lax.dynamic_slice_in_dim(mixed, index * group, group, 1)
        part_w = lax.dynamic_slice_in_dim(w_ot, index * group, group, 1)
        term = lax.dot_general(part_in, part_w, (((1,), (1,)), ((), ())), preferred_element_type=jnp.float32)
        rounded = lax.optimization_barrier(term.astype(jnp.bfloat16))
        return (total + rounded.astype(jnp.float32), None)
    total, _ = lax.scan(add_group, jnp.zeros((mixed.shape[0], D), jnp.float32), jnp.arange(N_TP, dtype=jnp.int32))
    return total.astype(jnp.bfloat16)

def reference(trainer_panels, panel_ids, first_tokens, second_tokens, norm_gain, kv_cache, block_table, lengths, move_list):
    weights = assemble(trainer_panels, panel_ids)
    kv_width = KVH * HD
    w_q = weights[:, :D]
    w_k = weights[:, D:D + kv_width]
    w_v = weights[:, D + kv_width:D + 2 * kv_width]
    w_ot = weights[:, D + 2 * kv_width:]
    nblk = R_DEV * MAXB
    devices = ROLLOUTS // R_DEV
    cache = kv_cache.reshape(devices * nblk, BLK, 2 * kv_width)
    table = block_table + (jnp.arange(ROLLOUTS, dtype=jnp.int32) // R_DEV * nblk)[:, None]
    table = table.astype(jnp.int32)
    outputs = []
    for step, tokens in enumerate((first_tokens, second_tokens)):
        values = tokens.astype(jnp.float32)
        scale = lax.rsqrt(lax.optimization_barrier(jnp.mean(values * values, axis=-1, keepdims=True)) + 1e-06)
        normed = (values * scale * norm_gain).astype(jnp.bfloat16)
        query = jnp.dot(normed, w_q, preferred_element_type=jnp.float32).astype(jnp.bfloat16)
        key = jnp.dot(normed, w_k, preferred_element_type=jnp.float32).astype(jnp.bfloat16)
        value = jnp.dot(normed, w_v, preferred_element_type=jnp.float32).astype(jnp.bfloat16)
        fresh = jnp.concatenate([key.reshape(ROLLOUTS, KVH, HD), value.reshape(ROLLOUTS, KVH, HD)], axis=2).reshape(ROLLOUTS, 2 * kv_width)
        position = (lengths + step).astype(jnp.int32)
        rows = jnp.take_along_axis(table, (position // BLK)[:, None], axis=1)[:, 0]
        cache = cache.at[rows, position % BLK].set(fresh)
        mixed = attend(query, cache, table, position + 1)
        outputs.append(project(mixed, w_ot))
    engine_ids = jnp.arange(N_ENGINE, dtype=jnp.int32)[:, None, None, None]
    rank_ids = jnp.arange(N_TP, dtype=jnp.int32)[None, :, None, None]
    valid = move_list < nblk
    rows = (engine_ids * N_TP + rank_ids) * nblk + jnp.where(valid, move_list, 0)
    picked = jnp.take(cache, rows.astype(jnp.int32), axis=0)
    picked = jnp.where(valid[..., None, None], picked, jnp.zeros((), jnp.bfloat16))
    hosted = jnp.transpose(picked, (2, 1, 0, 3, 4, 5)).reshape(N_ENGINE, N_TP * N_ENGINE * MSLOT, BLK, 2 * kv_width)
    return (outputs[0], outputs[1], hosted)
```

```python
import math

import jax
import jax.numpy as jnp
from jax import lax
from jax.experimental import pallas as pl
from jax.experimental.pallas import tpu as pltpu
from jax.sharding import Mesh
from jax.sharding import PartitionSpec as P

D = 8192
KVH = 8
HD = 128
PANELS = 128
BLK = 128
MAXB = 6
NBLK = 24
KV = KVH * HD
QKV = D + 2 * KV
HALF_IN = QKV // 2
HALF_O = D // 2
PR = 64
BF = jnp.bfloat16
F32 = jnp.float32
PARTS_IN = ((0, 1792), (1792, 1792), (3584, 1536))
PARTS_O = ((0, 1408), (1408, 1408), (2816, 1280))
ORDERS = (("y", "x", "z"), ("x", "z", "y"), ("z", "y", "x"))
POS = {"y": 0, "x": 1, "z": 2}
ROWS = 16
VMEM = 60 * 2**20


def shift(v, axis, k):
    return lax.ppermute(v, axis, [(i, (i + k) % 4) for i in range(4)])


def swap(v):
    return lax.ppermute(v, "c", [(0, 1), (1, 0)])


def absolute(rel, i):
    twice = jnp.concatenate([rel, rel], axis=0)
    return lax.dynamic_slice_in_dim(twice, (4 - i) % 4, 4, 0)


def reduce_ring(chunk, rows, axis):
    h = rows // 2
    far = chunk(2).astype(BF)
    from_left = shift(far[:h], axis, 1)
    from_right = shift(far[h:], axis, -1)
    right = chunk(1)
    right = jnp.concatenate([right[:h] + from_left.astype(F32), right[h:]], axis=0).astype(BF)
    left = chunk(3)
    left = jnp.concatenate([left[:h], left[h:] + from_right.astype(F32)], axis=0).astype(BF)
    a = shift(right, axis, 1)
    b = shift(left, axis, -1)
    return chunk(0) + a.astype(F32) + b.astype(F32)


def reduce_part(rows_in, w, order):
    i = lax.axis_index(order[0])
    flat = rows_in.reshape(4, 16 * ROWS, rows_in.shape[-1])

    def product(k):
        mine = lax.dynamic_index_in_dim(flat, (i + k) % 4, 0, keepdims=False)
        return jnp.dot(mine, w, preferred_element_type=F32)

    total = reduce_ring(product, 16 * ROWS, order[0]).astype(BF)
    for axis, rows in ((order[1], 4 * ROWS), (order[2], ROWS)):
        j = lax.axis_index(axis)
        split = total.reshape(4, rows, total.shape[-1])

        def own(k, split=split, j=j):
            return lax.dynamic_index_in_dim(split, (j + k) % 4, 0, keepdims=False).astype(F32)

        total = reduce_ring(own, rows, axis).astype(BF)
    return total


def gather_ring(v, axis):
    h = v.shape[0] // 2
    left = shift(v, axis, 1)
    right = shift(v, axis, -1)
    far_a = shift(left[:h], axis, 1)
    far_b = shift(right[h:], axis, -1)
    return v, right, jnp.concatenate([far_a, far_b], axis=0), left


def gather_part(v, w, order):
    for axis in (order[2], order[1]):
        rel = jnp.stack(gather_ring(v, axis))
        v = absolute(rel, lax.axis_index(axis)).reshape(-1, v.shape[-1])
    outs = [
        lax.dot_general(m, w, (((1,), (1,)), ((), ())), preferred_element_type=F32)
        for m in gather_ring(v, order[0])
    ]
    out = absolute(jnp.stack(outs), lax.axis_index(order[0]))
    out = out.reshape(4, 4, 4, ROWS, out.shape[-1])
    perm = [order.index(a) for a in ("y", "x", "z")]
    return out.transpose(*perm, 3, 4)


def pick_kernel(ids_ref, x_ref, scale_ref, gain_ref, out_ref):
    e = pl.program_id(0)
    lane = lax.broadcasted_iota(jnp.int32, (256, 128), 1)
    scale = scale_ref[...]

    def column(slot):
        p = ids_ref[e * 4 + slot]
        valid = p < PANELS
        p = jnp.where(valid, p, 0)
        at = pl.multiple_of((p // 2) * 128, 128)
        v = x_ref[:, pl.ds(at, 128)].astype(F32) * scale * gain_ref[:, pl.ds(at, 128)]
        v = jnp.where(valid, v, 0.0)
        return v, p % 2

    for pair in range(2):
        a, odd_a = column(2 * pair)
        b, odd_b = column(2 * pair + 1)
        a = jnp.where(odd_a == 1, pltpu.roll(a, 64, 1), a)
        b = jnp.where(odd_b == 0, pltpu.roll(b, 64, 1), b)
        both = jnp.where(lane < 64, a, b).astype(BF)
        out_ref[0, :, pair * 128 : (pair + 1) * 128] = both


def pick_columns(ids, x, scale, gain):
    return pl.pallas_call(
        pick_kernel,
        grid_spec=pltpu.PrefetchScalarGridSpec(
            num_scalar_prefetch=1,
            grid=(4,),
            in_specs=[
                pl.BlockSpec((256, D), lambda e, ids: (0, 0)),
                pl.BlockSpec((256, 1), lambda e, ids: (0, 0)),
                pl.BlockSpec((1, D), lambda e, ids: (0, 0)),
            ],
            out_specs=pl.BlockSpec((1, 256, 256), lambda e, ids: (e, 0, 0)),
        ),
        out_shape=jax.ShapeDtypeStruct((4, 256, 256), BF),
        compiler_params=pltpu.CompilerParams(vmem_limit_bytes=VMEM),
        name="pick_columns",
    )(ids, x, scale, gain)


def attend_kernel(table_ref, length_ref, q_ref, k_ref, v_ref, *refs):
    blocks, out_ref = refs[:MAXB], refs[MAXB]
    r = pl.program_id(0)
    length = length_ref[r]
    inverse_root = 1.0 / math.sqrt(HD)
    row = lax.broadcasted_iota(jnp.int32, (16, 128), 0)
    lane = lax.broadcasted_iota(jnp.int32, (16, 128), 1)
    fresh_seen = jnp.logical_or(lane == 0, jnp.logical_and(lane == 1, row >= 8))
    nt = (((1,), (1,)), ((), ()))
    pad = jnp.zeros((126, HD), F32)
    for g in range(KVH):
        lo = g * HD
        q = q_ref[0, g]
        new_k = jnp.concatenate([k_ref[0, :, lo : lo + HD].astype(F32), pad], axis=0).astype(BF)
        new_v = jnp.concatenate([v_ref[0, :, lo : lo + HD].astype(F32), pad], axis=0).astype(BF)
        scores = []
        for b in range(MAXB):
            keys = blocks[b][0, :, 2 * lo : 2 * lo + HD]
            s = lax.dot_general(q, keys, nt, preferred_element_type=F32) * inverse_root
            scores.append(jnp.where(lane + b * BLK < length, s, -1e30))
        s = lax.dot_general(q, new_k, nt, preferred_element_type=F32) * inverse_root
        scores.append(jnp.where(fresh_seen, s, -1e30))
        top = scores[0]
        for s in scores[1:]:
            top = jnp.maximum(top, s)
        top = jnp.max(top, axis=1, keepdims=True)
        weights = [jnp.exp(s - top) for s in scores]
        total = weights[0]
        for p in weights[1:]:
            total = total + p
        total = jnp.sum(total, axis=1, keepdims=True)
        inverse = 1.0 / total
        mixed = jnp.dot((weights[MAXB] * inverse).astype(BF), new_v, preferred_element_type=F32)
        for b in range(MAXB):
            vals = blocks[b][0, :, 2 * lo + HD : 2 * lo + 2 * HD]
            mixed += jnp.dot((weights[b] * inverse).astype(BF), vals, preferred_element_type=F32)
        out_ref[0, g] = mixed.astype(BF)


def attend(table, length, q, k, v, cache):
    def block(b):
        return pl.BlockSpec((1, BLK, 2 * KV), lambda r, t, n: (t[r * MAXB + b], 0, 0))

    return pl.pallas_call(
        attend_kernel,
        grid_spec=pltpu.PrefetchScalarGridSpec(
            num_scalar_prefetch=2,
            grid=(4,),
            in_specs=[
                pl.BlockSpec((1, KVH, 16, HD), lambda r, t, n: (r, 0, 0, 0)),
                pl.BlockSpec((1, 2, KV), lambda r, t, n: (r, 0, 0)),
                pl.BlockSpec((1, 2, KV), lambda r, t, n: (r, 0, 0)),
                *[block(b) for b in range(MAXB)],
            ],
            out_specs=pl.BlockSpec((1, KVH, 16, HD), lambda r, t, n: (r, 0, 0, 0)),
        ),
        out_shape=jax.ShapeDtypeStruct((4, KVH, 16, HD), BF),
        compiler_params=pltpu.CompilerParams(vmem_limit_bytes=VMEM),
        cost_estimate=pl.CostEstimate(flops=200_000_000, bytes_accessed=13_000_000, transcendentals=400_000),
        name="attend",
    )(table, length, q, k, v, *[cache] * MAXB)


def move_kernel(want_ref, table_ref, length_ref, fresh_ref, block_ref, out_ref):
    i = pl.program_id(0)
    b = want_ref[i]
    valid = b < NBLK
    out_ref[...] = jnp.where(valid, block_ref[...], jnp.zeros_like(block_ref))
    row = lax.broadcasted_iota(jnp.int32, (BLK, 2 * KV), 0)
    for r in range(4):
        for s in range(2):
            at = length_ref[r] + s
            hit = table_ref[r * MAXB + at // BLK] == b

            @pl.when(hit)
            def _(r=r, s=s, at=at):
                line = fresh_ref[2 * r + s : 2 * r + s + 1, :].astype(F32)
                old = out_ref[0].astype(F32)
                out_ref[0] = jnp.where(row == at % BLK, line, old).astype(BF)


def moved_blocks(want, table, length, fresh, cache):
    return pl.pallas_call(
        move_kernel,
        grid_spec=pltpu.PrefetchScalarGridSpec(
            num_scalar_prefetch=3,
            grid=(3,),
            in_specs=[
                pl.BlockSpec((8, 2 * KV), lambda i, w, t, n: (0, 0)),
                pl.BlockSpec((1, BLK, 2 * KV), lambda i, w, t, n: (jnp.minimum(w[i], NBLK - 1), 0, 0)),
            ],
            out_specs=pl.BlockSpec((1, BLK, 2 * KV), lambda i, w, t, n: (i, 0, 0)),
        ),
        out_shape=jax.ShapeDtypeStruct((3, BLK, 2 * KV), BF),
        compiler_params=pltpu.CompilerParams(vmem_limit_bytes=VMEM),
        cost_estimate=pl.CostEstimate(flops=1_000_000, bytes_accessed=3_200_000, transcendentals=0),
        name="moved_blocks",
    )(want, table, length, fresh, cache)


def order_kernel(chip_ref, half_ref, in_ref, out_ref):
    lane = lax.broadcasted_iota(jnp.int32, (ROWS, 128), 1)

    def side(p, low):
        v = in_ref[chip_ref[p]].astype(F32)
        half = half_ref[p]
        here = 0 if low else 1
        turned = pltpu.roll(v, 64, 1)
        v = jnp.where(half == here, v, turned)
        return jnp.where(half < 2, v, 0.0)

    def step(q, _):
        for s in range(2):
            pair = 2 * q + s
            both = jnp.where(lane < 64, side(2 * pair, True), side(2 * pair + 1, False))
            out_ref[q, :, s * 128 : (s + 1) * 128] = both.astype(BF)
        return 0

    lax.fori_loop(0, 32, step, 0)


def panel_order(chip, half, arrived):
    return pl.pallas_call(
        order_kernel,
        grid_spec=pltpu.PrefetchScalarGridSpec(
            num_scalar_prefetch=2,
            grid=(1,),
            in_specs=[pl.BlockSpec((64, ROWS, 128), lambda i, c, h: (0, 0, 0))],
            out_specs=pl.BlockSpec((32, ROWS, 256), lambda i, c, h: (0, 0, 0)),
        ),
        out_shape=jax.ShapeDtypeStruct((32, ROWS, 256), BF),
        name="panel_order",
    )(chip, half, arrived)


def per_device(panels, panel_ids, first, second, gain, kv_cache, block_table, lengths, move_list):
    y, c = lax.axis_index("y"), lax.axis_index("c")
    chip_xz = lax.axis_index("x") * 4 + lax.axis_index("z")
    cache = kv_cache[0]
    table = block_table.reshape(-1)

    ids = lax.all_to_all(
        jnp.broadcast_to(panel_ids[None], (128, 2)), ("y", "x", "z", "c"), 0, 0, tiled=True
    )
    ids = ids.reshape(4, 16, 2, 2)
    near = lax.dynamic_index_in_dim(ids, chip_xz, 1, keepdims=False)
    near = jnp.where(c == 0, near, near[:, ::-1]).reshape(16)

    w_in = panels[:, :, :QKV].reshape(2 * PR, QKV)
    w_o = panels[:, :, QKV:].reshape(2 * PR, D)
    keep_in = lax.dynamic_slice_in_dim(w_in, c * HALF_IN, HALF_IN, 1)
    give_in = lax.dynamic_slice_in_dim(w_in, (1 - c) * HALF_IN, HALF_IN, 1)
    keep_o = lax.dynamic_slice_in_dim(w_o, c * HALF_O, HALF_O, 1)
    give_o = lax.dynamic_slice_in_dim(w_o, (1 - c) * HALF_O, HALF_O, 1)
    w_in = jnp.concatenate([keep_in, swap(give_in)], axis=0)
    w_o = jnp.concatenate([keep_o, swap(give_o)], axis=0)

    tokens = jnp.stack([first.reshape(16, 8, D), second.reshape(16, 8, D)], axis=1).reshape(256, D)
    values = tokens.astype(F32)
    scale = lax.rsqrt(jnp.mean(values * values, axis=-1, keepdims=True) + 1e-06)
    picked = pick_columns(near, tokens, scale, gain.reshape(1, D))
    rows = lax.all_to_all(picked, "y", 0, 0, tiled=True).reshape(4, 4, 4, ROWS, 256)

    sums = []
    for (lo, width), order in zip(PARTS_IN, ORDERS):
        ordered = rows.transpose(*[POS[a] for a in order], 3, 4)
        sums.append(reduce_part(ordered, w_in[:, lo : lo + width], order))
    half = jnp.concatenate(sums, axis=1).reshape(2, 2, 4, HALF_IN)
    mine = lax.dynamic_index_in_dim(half, c, 1, keepdims=False).reshape(8, HALF_IN)
    other = swap(lax.dynamic_index_in_dim(half, 1 - c, 1, keepdims=False).reshape(8, HALF_IN))
    projected = jnp.where(
        c == 0, jnp.concatenate([mine, other], axis=1), jnp.concatenate([other, mine], axis=1)
    )
    projected = projected.reshape(2, 4, QKV)
    query = projected[:, :, :D].reshape(2, 4, KVH, 8, HD).transpose(1, 2, 0, 3, 4)
    query = query.reshape(4, KVH, 16, HD)
    new_k = projected[:, :, D : D + KV].transpose(1, 0, 2)
    new_v = projected[:, :, D + KV :].transpose(1, 0, 2)

    fresh = jnp.concatenate(
        [new_k.reshape(4, 2, KVH, HD), new_v.reshape(4, 2, KVH, HD)], axis=3
    ).reshape(8, 2 * KV)
    want = move_list.reshape(4)
    want = jnp.stack([lax.dynamic_index_in_dim(want, (y + k) % 4, 0, keepdims=False) for k in (1, 2, 3)])
    moving = moved_blocks(want, table, lengths, fresh, cache)
    got = [shift(moving[k - 1], "y", k) for k in (1, 2, 3)]

    mixed = attend(table, lengths, query, new_k, new_v, cache)
    mixed = mixed.reshape(4, KVH, 2, 8, HD).transpose(2, 0, 1, 3, 4).reshape(2, 1, 4, D)

    keep = lax.dynamic_slice_in_dim(mixed, c * HALF_O, HALF_O, 3)
    give = lax.dynamic_slice_in_dim(mixed, (1 - c) * HALF_O, HALF_O, 3)
    other = swap(give)
    mixed = jnp.where(
        c == 0, jnp.concatenate([keep, other], axis=1), jnp.concatenate([other, keep], axis=1)
    ).reshape(ROWS, HALF_O)
    out = 0
    for (lo, width), order in zip(PARTS_O, ORDERS):
        out = out + gather_part(mixed[:, lo : lo + width], w_o[:, lo : lo + width], order)
    out = out.reshape(64 * ROWS, 256)
    out = out[:, :128] + swap(out[:, 128:])

    arrived = lax.all_to_all(
        out.astype(BF).reshape(64, ROWS, 128), ("y", "x", "z"), 0, 0, tiled=True
    )
    flat = ids.reshape(256)
    match = flat[None, :] == jnp.arange(PANELS, dtype=jnp.int32)[:, None]
    slot = jnp.sum(jnp.where(match, jnp.arange(256, dtype=jnp.int32)[None, :], 0), axis=1)
    half_of = jnp.where((slot // 2) % 2 == c, slot % 2, 2)
    ordered = panel_order(slot // 4, half_of, arrived)
    final = lax.all_to_all(ordered, ("x", "z", "c"), 0, 0, tiled=True)
    final = final.reshape(16, 2, ROWS, 256)
    final = (final[:, 0] + final[:, 1]).reshape(16, 2, 8, 256)

    hosted = jnp.zeros((4, BLK, 2 * KV), BF)
    for k in (1, 2, 3):
        hosted = lax.dynamic_update_index_in_dim(hosted, got[k - 1], (y + 4 - k) % 4, 0)
    return final[:, 0].reshape(128, 256), final[:, 1].reshape(128, 256), hosted[None]


def solution(mesh):
    grid = Mesh(mesh.devices.reshape(4, 4, 4, 2), ("y", "x", "z", "c"))
    every, plane = ("y", "x", "z", "c"), ("x", "z", "c")
    placed = (
        P(every, None, None),
        P(every),
        P("y", None),
        P("y", None),
        P(),
        P("y", plane, None, None),
        P(every, None),
        P(every),
        P("y", plane, None, None),
    )
    return jax.shard_map(
        per_device,
        mesh=grid,
        in_specs=placed,
        out_specs=(P("y", plane), P("y", plane), P("y", plane, None, None)),
        check_vma=False,
    )
```

```python
import math

import jax
import jax.numpy as jnp
from jax import lax
from jax.experimental import pallas as pl
from jax.experimental.pallas import tpu as pltpu
from jax.sharding import Mesh
from jax.sharding import PartitionSpec as P

D = 8192
KVH = 8
HD = 128
PANELS = 128
BLK = 128
MAXB = 6
NBLK = 24
KV = KVH * HD
QKV = D + 2 * KV
GROUP = 1280
PR = 64
BF = jnp.bfloat16
F32 = jnp.float32
ROWS = 16
VMEM = 60 * 2**20


def shift(v, axis, k):
    return lax.ppermute(v, axis, [(i, (i + k) % 4) for i in range(4)])


def swap(v):
    return lax.ppermute(v, "c", [(0, 1), (1, 0)])


def split_kernel(q_ref, k_ref, v_ref, out_ref):
    for s in range(2):
        rows = slice(s * PR, (s + 1) * PR)
        out_ref[0, rows, :1024] = q_ref[s]
        out_ref[0, rows, 1024 : 1024 + HD] = k_ref[s]
        out_ref[0, rows, 1024 + HD :] = v_ref[s]


def split_heads(panels):
    return pl.pallas_call(
        split_kernel,
        grid=(KVH,),
        in_specs=[
            pl.BlockSpec((2, PR, 1024), lambda g: (0, 0, g)),
            pl.BlockSpec((2, PR, HD), lambda g: (0, 0, D // HD + g)),
            pl.BlockSpec((2, PR, HD), lambda g: (0, 0, (D + KV) // HD + g)),
        ],
        out_specs=pl.BlockSpec((1, 2 * PR, GROUP), lambda g: (g, 0, 0)),
        out_shape=jax.ShapeDtypeStruct((KVH, 2 * PR, GROUP), BF),
        cost_estimate=pl.CostEstimate(flops=0, bytes_accessed=5_300_000, transcendentals=0),
        name="split_heads",
    )(panels, panels, panels)


def pick_kernel(ids_ref, at_ref, first_ref, second_ref, gain_ref, out_ref, x_ref, scale_ref):
    e = pl.program_id(0)

    @pl.when(e == 0)
    def _():
        x = jnp.concatenate([first_ref[...].astype(F32), second_ref[...].astype(F32)], axis=0)
        x_ref[...] = x
        mean = jnp.mean(x * x, axis=-1, keepdims=True)
        scale_ref[...] = jnp.broadcast_to(lax.rsqrt(mean + 1e-06), (32, 128))

    lane = lax.broadcasted_iota(jnp.int32, (32, 128), 1)
    scale = scale_ref[...]
    new = lax.broadcasted_iota(jnp.int32, (32, 32), 0)
    old = lax.broadcasted_iota(jnp.int32, (32, 32), 1)
    source = ((new // 4) % 2) * 16 + (new // 8) * 4 + new % 4
    turn = (old == source).astype(BF)

    def column(slot):
        p = ids_ref[e * 16 + slot]
        valid = p < PANELS
        p = jnp.where(valid, p, 0)
        at = pl.multiple_of((p // 2) * 128, 128)
        v = x_ref[:, pl.ds(at, 128)] * scale * gain_ref[:, pl.ds(at, 128)]
        return jnp.where(valid, v, 0.0), p % 2

    for pair in range(8):
        a, odd_a = column(2 * pair)
        b, odd_b = column(2 * pair + 1)
        a = jnp.where(odd_a == 1, pltpu.roll(a, 64, 1), a)
        b = jnp.where(odd_b == 0, pltpu.roll(b, 64, 1), b)
        both = jnp.where(lane < 64, a, b).astype(BF)
        both = jnp.dot(turn, both, preferred_element_type=F32).astype(BF)
        for z in range(4):
            out_ref[0, z, :, pair * 128 : (pair + 1) * 128] = both


def pick_columns(ids, at, first, second, gain):
    return pl.pallas_call(
        pick_kernel,
        grid_spec=pltpu.PrefetchScalarGridSpec(
            num_scalar_prefetch=2,
            grid=(4,),
            in_specs=[
                pl.BlockSpec((16, D), lambda e, ids, at: (at[0], 0)),
                pl.BlockSpec((16, D), lambda e, ids, at: (at[0], 0)),
                pl.BlockSpec((1, D), lambda e, ids, at: (0, 0)),
            ],
            out_specs=pl.BlockSpec((1, 4, 32, 1024), lambda e, ids, at: (e, 0, 0, 0)),
            scratch_shapes=[pltpu.VMEM((32, D), F32), pltpu.VMEM((32, 128), F32)],
        ),
        out_shape=jax.ShapeDtypeStruct((4, 4, 32, 1024), BF),
        cost_estimate=pl.CostEstimate(flops=20_000_000, bytes_accessed=2_000_000, transcendentals=0),
        name="pick_columns",
    )(ids, at, first, second, gain)


def attend_kernel(table_ref, length_ref, q_ref, k_ref, v_ref, *refs):
    blocks, out_ref = refs[:MAXB], refs[MAXB]
    r = pl.program_id(0)
    length = length_ref[r]
    inverse_root = 1.0 / math.sqrt(HD)
    row = lax.broadcasted_iota(jnp.int32, (16, 128), 0)
    lane = lax.broadcasted_iota(jnp.int32, (16, 128), 1)
    fresh_seen = jnp.logical_or(lane == 0, jnp.logical_and(lane == 1, row >= 8))
    nt = (((1,), (1,)), ((), ()))
    pad = jnp.zeros((126, HD), F32)
    for g in range(KVH):
        lo = g * HD
        q = q_ref[0, g]
        new_k = jnp.concatenate([k_ref[0, :, lo : lo + HD].astype(F32), pad], axis=0).astype(BF)
        new_v = jnp.concatenate([v_ref[0, :, lo : lo + HD].astype(F32), pad], axis=0).astype(BF)
        scores = []
        for b in range(MAXB):
            keys = blocks[b][0, :, 2 * lo : 2 * lo + HD]
            s = lax.dot_general(q, keys, nt, preferred_element_type=F32) * inverse_root
            scores.append(jnp.where(lane + b * BLK < length, s, -1e30))
        s = lax.dot_general(q, new_k, nt, preferred_element_type=F32) * inverse_root
        scores.append(jnp.where(fresh_seen, s, -1e30))
        top = scores[0]
        for s in scores[1:]:
            top = jnp.maximum(top, s)
        top = jnp.max(top, axis=1, keepdims=True)
        weights = [jnp.exp(s - top) for s in scores]
        total = weights[0]
        for p in weights[1:]:
            total = total + p
        total = jnp.sum(total, axis=1, keepdims=True)
        inverse = 1.0 / total
        mixed = jnp.dot((weights[MAXB] * inverse).astype(BF), new_v, preferred_element_type=F32)
        for b in range(MAXB):
            vals = blocks[b][0, :, 2 * lo + HD : 2 * lo + 2 * HD]
            mixed += jnp.dot((weights[b] * inverse).astype(BF), vals, preferred_element_type=F32)
        out_ref[0, g] = mixed.astype(BF)


def attend(table, length, q, k, v, cache):
    def block(b):
        return pl.BlockSpec((1, BLK, 2 * KV), lambda r, t, n: (t[r * MAXB + b], 0, 0))

    return pl.pallas_call(
        attend_kernel,
        grid_spec=pltpu.PrefetchScalarGridSpec(
            num_scalar_prefetch=2,
            grid=(4,),
            in_specs=[
                pl.BlockSpec((1, KVH, 16, HD), lambda r, t, n: (r, 0, 0, 0)),
                pl.BlockSpec((1, 2, KV), lambda r, t, n: (r, 0, 0)),
                pl.BlockSpec((1, 2, KV), lambda r, t, n: (r, 0, 0)),
                *[block(b) for b in range(MAXB)],
            ],
            out_specs=pl.BlockSpec((1, KVH, 16, HD), lambda r, t, n: (r, 0, 0, 0)),
        ),
        out_shape=jax.ShapeDtypeStruct((4, KVH, 16, HD), BF),
        compiler_params=pltpu.CompilerParams(vmem_limit_bytes=VMEM),
        cost_estimate=pl.CostEstimate(flops=200_000_000, bytes_accessed=13_000_000, transcendentals=400_000),
        name="attend",
    )(table, length, q, k, v, *[cache] * MAXB)


def move_kernel(want_ref, table_ref, length_ref, fresh_ref, block_ref, out_ref):
    i = pl.program_id(0)
    b = want_ref[i]
    valid = b < NBLK
    out_ref[...] = jnp.where(valid, block_ref[...], jnp.zeros_like(block_ref))
    row = lax.broadcasted_iota(jnp.int32, (BLK, 2 * KV), 0)
    for r in range(4):
        for s in range(2):
            at = length_ref[r] + s
            hit = table_ref[r * MAXB + at // BLK] == b

            @pl.when(hit)
            def _(r=r, s=s, at=at):
                line = fresh_ref[2 * r + s : 2 * r + s + 1, :].astype(F32)
                old = out_ref[0].astype(F32)
                out_ref[0] = jnp.where(row == at % BLK, line, old).astype(BF)


def moved_blocks(want, table, length, fresh, cache):
    return pl.pallas_call(
        move_kernel,
        grid_spec=pltpu.PrefetchScalarGridSpec(
            num_scalar_prefetch=3,
            grid=(3,),
            in_specs=[
                pl.BlockSpec((8, 2 * KV), lambda i, w, t, n: (0, 0)),
                pl.BlockSpec((1, BLK, 2 * KV), lambda i, w, t, n: (jnp.minimum(w[i], NBLK - 1), 0, 0)),
            ],
            out_specs=pl.BlockSpec((1, BLK, 2 * KV), lambda i, w, t, n: (i, 0, 0)),
        ),
        out_shape=jax.ShapeDtypeStruct((3, BLK, 2 * KV), BF),
        compiler_params=pltpu.CompilerParams(vmem_limit_bytes=VMEM),
        cost_estimate=pl.CostEstimate(flops=1_000_000, bytes_accessed=3_200_000, transcendentals=0),
        name="moved_blocks",
    )(want, table, length, fresh, cache)


def order_kernel(from_ref, at_ref, half_ref, in_ref, out_ref):
    lane = lax.broadcasted_iota(jnp.int32, (8, 128), 1)

    def side(p, here):
        at = pl.multiple_of(at_ref[p] * 128, 128)
        v = in_ref[from_ref[p], :, pl.ds(at, 128)].astype(F32)
        return jnp.where(half_ref[p] == here, v, pltpu.roll(v, 64, 1))

    def step(q, _):
        for s in range(2):
            pair = 2 * q + s
            both = jnp.where(lane < 64, side(2 * pair, 0), side(2 * pair + 1, 1))
            out_ref[q, :, s * 128 : (s + 1) * 128] = both.astype(BF)
        return 0

    lax.fori_loop(0, 32, step, 0)


def panel_order(source, at, half, arrived):
    return pl.pallas_call(
        order_kernel,
        grid_spec=pltpu.PrefetchScalarGridSpec(
            num_scalar_prefetch=3,
            grid=(1,),
            in_specs=[pl.BlockSpec((32, 8, 512), lambda i, f, a, h: (0, 0, 0))],
            out_specs=pl.BlockSpec((32, 8, 256), lambda i, f, a, h: (0, 0, 0)),
        ),
        out_shape=jax.ShapeDtypeStruct((32, 8, 256), BF),
        name="panel_order",
    )(source, at, half, arrived)


def per_device(panels, panel_ids, first, second, gain, kv_cache, block_table, lengths, move_list):
    y, x = lax.axis_index("y"), lax.axis_index("x")
    z, c = lax.axis_index("z"), lax.axis_index("c")
    cache = kv_cache[0]
    table = block_table.reshape(-1)
    plane = ("x", "z", "c")

    w_o = lax.all_gather(panels[:, :, QKV:], "y", axis=0, tiled=True).reshape(8 * PR, D)

    ids = lax.all_to_all(
        jnp.broadcast_to(panel_ids[None], (128, 2)), ("y", "x", "z", "c"), 0, 0, tiled=True
    )
    near = lax.dynamic_index_in_dim(ids.reshape(4, 4, 16), x, 1, keepdims=False).reshape(64)

    w_in = lax.all_to_all(split_heads(panels), ("z", "c"), 0, 0, tiled=True).reshape(16 * PR, GROUP)

    block = (z * 2 + c).reshape(1)
    picked = pick_columns(near, block, first, second, gain.reshape(1, D))
    rows = lax.all_to_all(picked.reshape(16, 32, 1024), ("y", "z"), 0, 0, tiled=True)
    other = swap(rows)
    rows = jnp.where(
        c == 0, jnp.stack([rows, other], axis=1), jnp.stack([other, rows], axis=1)
    ).reshape(64 * ROWS, 1024)
    partial = jnp.dot(rows, w_in, preferred_element_type=F32).astype(BF)
    parts = lax.all_to_all(partial.reshape(16, 64, GROUP), ("y", "x"), 0, 0, tiled=True)
    summed = jnp.sum(parts.astype(F32), axis=0).astype(BF)
    projected = lax.all_to_all(summed.reshape(8, 8, GROUP), ("z", "c"), 0, 0, tiled=True)
    projected = projected.reshape(KVH, 2, 4, GROUP)
    query = projected[..., :1024].reshape(KVH, 2, 4, 8, HD).transpose(2, 0, 1, 3, 4)
    query = query.reshape(4, KVH, 16, HD)
    fresh = projected[..., 1024:].transpose(2, 1, 0, 3)
    new_k = fresh[..., :HD].reshape(4, 2, KV)
    new_v = fresh[..., HD:].reshape(4, 2, KV)
    fresh = fresh.reshape(8, 2 * KV)

    want = move_list.reshape(4)
    want = jnp.stack([lax.dynamic_index_in_dim(want, (y + k) % 4, 0, keepdims=False) for k in (1, 2, 3)])
    moving = moved_blocks(want, table, lengths, fresh, cache)
    got = [shift(moving[k - 1], "y", k) for k in (1, 2, 3)]

    mixed = attend(table, lengths, query, new_k, new_v, cache)
    mixed = mixed.reshape(4, KVH, 2, 8, HD).transpose(2, 0, 1, 3, 4).reshape(8, D)
    mixed = lax.all_gather(mixed, plane, axis=0, tiled=True)
    out = lax.dot_general(mixed, w_o, (((1,), (1,)), ((), ())), preferred_element_type=F32)

    arrived = lax.all_to_all(out.astype(BF).reshape(32, 8, 512), plane, 0, 0, tiled=True)
    match = ids.reshape(1, 256) == jnp.arange(PANELS, dtype=jnp.int32)[:, None]
    slot = jnp.sum(jnp.where(match, jnp.arange(256, dtype=jnp.int32)[None, :], 0), axis=1)
    ordered = panel_order((slot // 2) % 32, slot // 64, slot % 2, arrived)
    final = lax.all_to_all(ordered, plane, 0, 0, tiled=True).reshape(32, 2, 4, 256)

    hosted = jnp.zeros((4, BLK, 2 * KV), BF)
    for k in (1, 2, 3):
        hosted = lax.dynamic_update_index_in_dim(hosted, got[k - 1], (y + 4 - k) % 4, 0)
    return final[:, 0].reshape(128, 256), final[:, 1].reshape(128, 256), hosted[None]


def solution(mesh):
    grid = Mesh(mesh.devices.reshape(4, 4, 4, 2), ("y", "x", "z", "c"))
    every, plane = ("y", "x", "z", "c"), ("x", "z", "c")
    placed = (
        P(every, None, None),
        P(every),
        P("y", None),
        P("y", None),
        P(),
        P("y", plane, None, None),
        P(every, None),
        P(every),
        P("y", plane, None, None),
    )
    return jax.shard_map(
        per_device,
        mesh=grid,
        in_specs=placed,
        out_specs=(P("y", plane), P("y", plane), P("y", plane, None, None)),
        check_vma=False,
    )
```

```python
import math

import jax
import jax.numpy as jnp
from jax import lax
from jax.experimental import pallas as pl
from jax.experimental.pallas import tpu as pltpu
from jax.sharding import Mesh
from jax.sharding import PartitionSpec as P

D = 8192
KVH = 8
HD = 128
PANELS = 128
BLK = 128
MAXB = 6
NBLK = 24
KV = KVH * HD
QKV = D + 2 * KV
GROUP = 1280
PR = 64
BF = jnp.bfloat16
F32 = jnp.float32
ROWS = 16
FIRST, LAST = (0, 2, 3, 4, 6, 7), (1, 2, 3, 5, 6, 7)
VMEM = 60 * 2**20


def shift(v, axis, k):
    return lax.ppermute(v, axis, [(i, (i + k) % 4) for i in range(4)])


def swap(v):
    return lax.ppermute(v, "c", [(0, 1), (1, 0)])


def split_kernel(place_ref, q_ref, k_ref, v_ref, *outs):
    step = pl.program_id(0)
    for out_ref, first, last in zip(outs, FIRST, LAST):

        @pl.when(jnp.logical_and(step >= first, step <= last))
        def _(out_ref=out_ref):
            for s in range(2):
                rows = slice(s * PR, (s + 1) * PR)
                out_ref[0, rows, :1024] = q_ref[s]
                out_ref[0, rows, 1024 : 1024 + HD] = k_ref[s]
                out_ref[0, rows, 1024 + HD :] = v_ref[s]


def split_heads(place, panels):
    def group(k, p):
        core = jnp.where(jnp.logical_or(k == 3, jnp.logical_or(k == 1, jnp.logical_or(k == 5, k == 7))), 1, 0)
        return lax.rem(p[0] + k // 2 + 1, 4) * 2 + lax.rem(p[1] + core, 2)

    def piece(first, last):
        return pl.BlockSpec(
            (1, 2 * PR, GROUP), lambda k, p: (jnp.clip(k, first, last) - first, 0, 0)
        )

    return pl.pallas_call(
        split_kernel,
        grid_spec=pltpu.PrefetchScalarGridSpec(
            num_scalar_prefetch=1,
            grid=(8,),
            in_specs=[
                pl.BlockSpec((2, PR, 1024), lambda k, p: (0, 0, group(k, p))),
                pl.BlockSpec((2, PR, HD), lambda k, p: (0, 0, D // HD + group(k, p))),
                pl.BlockSpec((2, PR, HD), lambda k, p: (0, 0, (D + KV) // HD + group(k, p))),
            ],
            out_specs=[piece(a, b) for a, b in zip(FIRST, LAST)],
        ),
        out_shape=[jax.ShapeDtypeStruct((n, 2 * PR, GROUP), BF) for n in (2, 1, 1, 2, 1, 1)],
        cost_estimate=pl.CostEstimate(flops=0, bytes_accessed=5_300_000, transcendentals=0),
        name="split_heads",
    )(place, panels, panels, panels)


def project_kernel(core_ref, mine_ref, other_ref, *refs):
    pieces, (out_ref, w_ref) = refs[:8], refs[8:]
    core = core_ref[0]

    @pl.when(pl.program_id(0) == 0)
    def _():
        for i, piece in enumerate(pieces):
            slot = jnp.where(i % 2 == 0, core, 1 - core)
            at = pl.multiple_of((i // 2) * 256 + slot * 128, 128)
            w_ref[pl.ds(at, 128), :] = piece[0]

    mine, other = mine_ref[...], other_ref[...]
    low = core == 0
    x = jnp.concatenate([jnp.where(low, mine, other), jnp.where(low, other, mine)], axis=1)
    x = x.reshape(256, 1024)
    for lo in range(0, GROUP, 256):
        total = jnp.dot(x, w_ref[:, lo : lo + 256], preferred_element_type=F32)
        out_ref[:, :, lo : lo + 256] = total.reshape(4, 64, 256).astype(BF)


def project(core, mine, other, *pieces):
    rows = pl.BlockSpec((4, 32, 1024), lambda i, c: (i, 0, 0))
    return pl.pallas_call(
        project_kernel,
        grid_spec=pltpu.PrefetchScalarGridSpec(
            num_scalar_prefetch=1,
            grid=(4,),
            in_specs=[
                rows,
                rows,
                *[pl.BlockSpec((1, 2 * PR, GROUP), lambda i, c, at=at: (at, 0, 0)) for _, at in pieces],
            ],
            out_specs=pl.BlockSpec((4, 64, GROUP), lambda i, c: (i, 0, 0)),
            scratch_shapes=[pltpu.VMEM((16 * PR, GROUP), BF)],
        ),
        out_shape=jax.ShapeDtypeStruct((16, 64, GROUP), BF),
        compiler_params=pltpu.CompilerParams(vmem_limit_bytes=VMEM),
        cost_estimate=pl.CostEstimate(flops=2_700_000_000, bytes_accessed=7_500_000, transcendentals=0),
        name="project",
    )(core, mine, other, *[v for v, _ in pieces])


def output_kernel(x_ref, *refs):
    pieces, (out_ref, sum_ref) = refs[:8], refs[8:]
    k = pl.program_id(0)

    @pl.when(k == 0)
    def _():
        sum_ref[...] = jnp.zeros_like(sum_ref)

    w = jnp.concatenate([r[0] for r in pieces], axis=0)
    sum_ref[...] += lax.dot_general(x_ref[...], w, (((1,), (1,)), ((), ())), preferred_element_type=F32)

    @pl.when(k == pl.num_programs(0) - 1)
    def _():
        out_ref[...] = sum_ref[...].reshape(32, 8, 512).astype(BF)


def output_product(x, w):
    return pl.pallas_call(
        output_kernel,
        grid=(4,),
        in_specs=[
            pl.BlockSpec((256, 2048), lambda k: (0, k)),
            *[pl.BlockSpec((1, PR, 2048), lambda k, i=i: (i, 0, k)) for i in range(8)],
        ],
        out_specs=pl.BlockSpec((32, 8, 512), lambda k: (0, 0, 0)),
        out_shape=jax.ShapeDtypeStruct((32, 8, 512), BF),
        scratch_shapes=[pltpu.VMEM((256, 512), F32)],
        compiler_params=pltpu.CompilerParams(vmem_limit_bytes=VMEM),
        cost_estimate=pl.CostEstimate(flops=2_150_000_000, bytes_accessed=12_800_000, transcendentals=0),
        name="output_product",
    )(x, *[w] * 8)


def pick_kernel(ids_ref, at_ref, first_ref, second_ref, gain_ref, out_ref, x_ref, scale_ref):
    e = pl.program_id(0)

    @pl.when(e == 0)
    def _():
        x = jnp.concatenate([first_ref[...].astype(F32), second_ref[...].astype(F32)], axis=0)
        x_ref[...] = x
        mean = jnp.mean(x * x, axis=-1, keepdims=True)
        scale_ref[...] = jnp.broadcast_to(lax.rsqrt(mean + 1e-06), (32, 128))

    lane = lax.broadcasted_iota(jnp.int32, (32, 128), 1)
    scale = scale_ref[...]
    new = lax.broadcasted_iota(jnp.int32, (32, 32), 0)
    old = lax.broadcasted_iota(jnp.int32, (32, 32), 1)
    source = ((new // 4) % 2) * 16 + (new // 8) * 4 + new % 4
    turn = (old == source).astype(BF)

    def column(slot):
        p = ids_ref[e * 16 + slot]
        valid = p < PANELS
        p = jnp.where(valid, p, 0)
        at = pl.multiple_of((p // 2) * 128, 128)
        v = x_ref[:, pl.ds(at, 128)] * scale * gain_ref[:, pl.ds(at, 128)]
        return jnp.where(valid, v, 0.0), p % 2

    for pair in range(8):
        a, odd_a = column(2 * pair)
        b, odd_b = column(2 * pair + 1)
        a = jnp.where(odd_a == 1, pltpu.roll(a, 64, 1), a)
        b = jnp.where(odd_b == 0, pltpu.roll(b, 64, 1), b)
        both = jnp.where(lane < 64, a, b).astype(BF)
        both = jnp.dot(turn, both, preferred_element_type=F32).astype(BF)
        for z in range(4):
            at = (pair // 2 - z) % 4 * 256 + pair % 2 * 128
            out_ref[0, z, :, at : at + 128] = both


def pick_columns(ids, at, first, second, gain):
    return pl.pallas_call(
        pick_kernel,
        grid_spec=pltpu.PrefetchScalarGridSpec(
            num_scalar_prefetch=2,
            grid=(4,),
            in_specs=[
                pl.BlockSpec((16, D), lambda e, ids, at: (at[0], 0)),
                pl.BlockSpec((16, D), lambda e, ids, at: (at[0], 0)),
                pl.BlockSpec((1, D), lambda e, ids, at: (0, 0)),
            ],
            out_specs=pl.BlockSpec((1, 4, 32, 1024), lambda e, ids, at: (e, 0, 0, 0)),
            scratch_shapes=[pltpu.VMEM((32, D), F32), pltpu.VMEM((32, 128), F32)],
        ),
        out_shape=jax.ShapeDtypeStruct((4, 4, 32, 1024), BF),
        cost_estimate=pl.CostEstimate(flops=20_000_000, bytes_accessed=2_000_000, transcendentals=0),
        name="pick_columns",
    )(ids, at, first, second, gain)


def attend_kernel(table_ref, length_ref, q_ref, k_ref, v_ref, *refs):
    blocks, (out_ref, score_ref, prob_ref, sum_ref) = refs[:MAXB], refs[MAXB:]
    r = pl.program_id(0)
    length = length_ref[r]
    inverse_root = 1.0 / math.sqrt(HD)
    lane = lax.broadcasted_iota(jnp.int32, (16, 128), 1)
    row = lax.broadcasted_iota(jnp.int32, (16, 128), 0)
    fresh_seen = jnp.logical_or(lane == 0, jnp.logical_and(lane == 1, row >= 8))
    nt = (((1,), (1,)), ((), ()))
    pad = jnp.zeros((126, HD), F32)

    for b in range(MAXB):
        seen = b * BLK < length

        @pl.when(seen)
        def _(b=b):
            for g in range(KVH):
                keys = blocks[b][0, :, 2 * g * HD : (2 * g + 1) * HD]
                s = lax.dot_general(q_ref[0, g], keys, nt, preferred_element_type=F32) * inverse_root
                score_ref[b, g * 16 : (g + 1) * 16] = jnp.where(lane + b * BLK < length, s, -1e30)

        @pl.when(jnp.logical_not(seen))
        def _(b=b):
            score_ref[b] = jnp.full((128, 128), -1e30, F32)

    for g in range(KVH):
        new_k = jnp.concatenate([k_ref[0, :, g * HD : (g + 1) * HD].astype(F32), pad], axis=0)
        s = lax.dot_general(q_ref[0, g], new_k.astype(BF), nt, preferred_element_type=F32) * inverse_root
        score_ref[MAXB, g * 16 : (g + 1) * 16] = jnp.where(fresh_seen, s, -1e30)

    for g in range(KVH):
        rows = slice(g * 16, (g + 1) * 16)
        scores = [score_ref[b, rows] for b in range(MAXB + 1)]
        top = scores[0]
        for s in scores[1:]:
            top = jnp.maximum(top, s)
        top = jnp.max(top, axis=1, keepdims=True)
        weights = [jnp.exp(s - top) for s in scores]
        total = weights[0]
        for p in weights[1:]:
            total = total + p
        inverse = 1.0 / jnp.sum(total, axis=1, keepdims=True)
        for b in range(MAXB + 1):
            prob_ref[b, rows] = (weights[b] * inverse).astype(BF)

    for g in range(KVH):
        rows = slice(g * 16, (g + 1) * 16)
        new_v = jnp.concatenate([v_ref[0, :, g * HD : (g + 1) * HD].astype(F32), pad], axis=0)
        sum_ref[rows] = jnp.dot(prob_ref[MAXB, rows], new_v.astype(BF), preferred_element_type=F32)

    for b in range(MAXB):

        @pl.when(b * BLK < length)
        def _(b=b):
            for g in range(KVH):
                rows = slice(g * 16, (g + 1) * 16)
                vals = blocks[b][0, :, (2 * g + 1) * HD : (2 * g + 2) * HD]
                sum_ref[rows] += jnp.dot(prob_ref[b, rows], vals, preferred_element_type=F32)

    out_ref[0] = sum_ref[...].reshape(KVH, 16, HD).astype(BF)


def attend(table, length, q, k, v, cache):
    def block(b):
        return pl.BlockSpec((1, BLK, 2 * KV), lambda r, t, n: (t[r * MAXB + b], 0, 0))

    return pl.pallas_call(
        attend_kernel,
        grid_spec=pltpu.PrefetchScalarGridSpec(
            num_scalar_prefetch=2,
            grid=(4,),
            in_specs=[
                pl.BlockSpec((1, KVH, 16, HD), lambda r, t, n: (r, 0, 0, 0)),
                pl.BlockSpec((1, 2, KV), lambda r, t, n: (r, 0, 0)),
                pl.BlockSpec((1, 2, KV), lambda r, t, n: (r, 0, 0)),
                *[block(b) for b in range(MAXB)],
            ],
            out_specs=pl.BlockSpec((1, KVH, 16, HD), lambda r, t, n: (r, 0, 0, 0)),
            scratch_shapes=[
                pltpu.VMEM((MAXB + 1, 128, 128), F32),
                pltpu.VMEM((MAXB + 1, 128, 128), BF),
                pltpu.VMEM((128, HD), F32),
            ],
        ),
        out_shape=jax.ShapeDtypeStruct((4, KVH, 16, HD), BF),
        compiler_params=pltpu.CompilerParams(vmem_limit_bytes=VMEM),
        cost_estimate=pl.CostEstimate(flops=200_000_000, bytes_accessed=13_000_000, transcendentals=400_000),
        name="attend",
    )(table, length, q, k, v, *[cache] * MAXB)


def move_kernel(want_ref, table_ref, length_ref, fresh_ref, block_ref, out_ref):
    i = pl.program_id(0)
    b = want_ref[i]
    valid = b < NBLK
    out_ref[...] = jnp.where(valid, block_ref[...], jnp.zeros_like(block_ref))
    row = lax.broadcasted_iota(jnp.int32, (BLK, 2 * KV), 0)
    for r in range(4):
        for s in range(2):
            at = length_ref[r] + s
            hit = table_ref[r * MAXB + at // BLK] == b

            @pl.when(hit)
            def _(r=r, s=s, at=at):
                line = fresh_ref[2 * r + s : 2 * r + s + 1, :].astype(F32)
                old = out_ref[0].astype(F32)
                out_ref[0] = jnp.where(row == at % BLK, line, old).astype(BF)


def moved_blocks(want, table, length, fresh, cache):
    return pl.pallas_call(
        move_kernel,
        grid_spec=pltpu.PrefetchScalarGridSpec(
            num_scalar_prefetch=3,
            grid=(3,),
            in_specs=[
                pl.BlockSpec((8, 2 * KV), lambda i, w, t, n: (0, 0)),
                pl.BlockSpec((1, BLK, 2 * KV), lambda i, w, t, n: (jnp.minimum(w[i], NBLK - 1), 0, 0)),
            ],
            out_specs=pl.BlockSpec((1, BLK, 2 * KV), lambda i, w, t, n: (i, 0, 0)),
        ),
        out_shape=jax.ShapeDtypeStruct((3, BLK, 2 * KV), BF),
        compiler_params=pltpu.CompilerParams(vmem_limit_bytes=VMEM),
        cost_estimate=pl.CostEstimate(flops=1_000_000, bytes_accessed=3_200_000, transcendentals=0),
        name="moved_blocks",
    )(want, table, length, fresh, cache)


def order_kernel(from_ref, at_ref, half_ref, in_ref, out_ref):
    lane = lax.broadcasted_iota(jnp.int32, (8, 128), 1)

    def side(p, here):
        at = pl.multiple_of(at_ref[p] * 128, 128)
        v = in_ref[from_ref[p], :, pl.ds(at, 128)].astype(F32)
        return jnp.where(half_ref[p] == here, v, pltpu.roll(v, 64, 1))

    def step(q, _):
        for s in range(2):
            pair = 2 * q + s
            both = jnp.where(lane < 64, side(2 * pair, 0), side(2 * pair + 1, 1))
            out_ref[q, :, s * 128 : (s + 1) * 128] = both.astype(BF)
        return 0

    lax.fori_loop(0, 32, step, 0, unroll=4)


def panel_order(source, at, half, arrived):
    return pl.pallas_call(
        order_kernel,
        grid_spec=pltpu.PrefetchScalarGridSpec(
            num_scalar_prefetch=3,
            grid=(1,),
            in_specs=[pl.BlockSpec((32, 8, 512), lambda i, f, a, h: (0, 0, 0))],
            out_specs=pl.BlockSpec((32, 8, 256), lambda i, f, a, h: (0, 0, 0)),
        ),
        out_shape=jax.ShapeDtypeStruct((32, 8, 256), BF),
        name="panel_order",
    )(source, at, half, arrived)


def per_device(panels, panel_ids, first, second, gain, kv_cache, block_table, lengths, move_list):
    y, x = lax.axis_index("y"), lax.axis_index("x")
    z, c = lax.axis_index("z"), lax.axis_index("c")
    cache = kv_cache[0]
    table = block_table.reshape(-1)
    plane = ("x", "z", "c")

    right, far_a, far_b, left, own_a, own_b = split_heads(jnp.stack([z, c]), panels)
    own_b = swap(own_b)

    near = lax.all_to_all(
        jnp.broadcast_to(panel_ids, (32, 8, 64, 2)).reshape(32, 8, 128), ("y", "z", "c"), 0, 0, tiled=True
    )[:, 0, :2].reshape(64)
    near, right, left, far_a, far_b, w_o = lax.optimization_barrier(
        (near, right, left, far_a, far_b, panels[:, :, QKV:])
    )
    w_o = lax.all_gather(w_o, "y", axis=0, tiled=True)
    far_a = shift(far_a, "z", 1)
    far_b = shift(far_b, "z", -1)
    from_left = shift(right, "z", 1)
    from_right = shift(left, "z", -1)

    block = (z * 2 + c).reshape(1)
    picked = pick_columns(near, block, first, second, gain.reshape(1, D)).reshape(16, 32, 1024)
    picked, far_a, far_b = lax.optimization_barrier((picked, far_a, far_b))
    far_a = shift(far_a, "z", 1)
    far_b = shift(far_b, "z", -1)
    rows = lax.all_to_all(picked, ("y", "z"), 0, 0, tiled=True)
    rows, from_left, from_right, far_a, far_b = lax.optimization_barrier(
        (rows, from_left, from_right, far_a, far_b)
    )
    left_b = swap(from_left[1:])
    right_b = swap(from_right[1:])
    partial = project(
        c.reshape(1),
        rows,
        swap(rows),
        (own_a, 0),
        (own_b, 0),
        (from_right, 0),
        (right_b, 0),
        (far_a, 0),
        (swap(far_b), 0),
        (from_left, 0),
        (left_b, 0),
    )
    parts = lax.all_to_all(partial, ("y", "x"), 0, 0, tiled=True)
    summed = jnp.sum(parts.astype(F32), axis=0).astype(BF)
    projected = lax.all_to_all(summed.reshape(8, 8, GROUP), ("z", "c"), 0, 0, tiled=True)
    projected = projected.reshape(KVH, 2, 4, GROUP)
    query = projected[..., :1024].reshape(KVH, 2, 4, 8, HD).transpose(2, 0, 1, 3, 4)
    query = query.reshape(4, KVH, 16, HD)
    fresh = projected[..., 1024:].transpose(2, 1, 0, 3)
    new_k = fresh[..., :HD].reshape(4, 2, KV)
    new_v = fresh[..., HD:].reshape(4, 2, KV)
    fresh = fresh.reshape(8, 2 * KV)

    want = move_list.reshape(4)
    want = jnp.stack([lax.dynamic_index_in_dim(want, (y + k) % 4, 0, keepdims=False) for k in (1, 2, 3)])
    moving = moved_blocks(want, table, lengths, fresh, cache)
    got = [shift(moving[k - 1], "y", k) for k in (1, 2, 3)]
    mixed = attend(table, lengths, query, new_k, new_v, cache)
    mixed = mixed.reshape(4, KVH, 2, 8, HD).transpose(2, 0, 1, 3, 4).reshape(8, D)
    mixed, near = lax.optimization_barrier((mixed, near))
    mixed = lax.all_gather(mixed, plane, axis=0, tiled=True)
    out = output_product(mixed, w_o)

    ids = lax.all_to_all(jnp.broadcast_to(near[None], (4, 64)), "x", 0, 0, tiled=True)
    match = ids.reshape(1, 256) == jnp.arange(PANELS, dtype=jnp.int32)[:, None]
    slot = jnp.sum(jnp.where(match, jnp.arange(256, dtype=jnp.int32)[None, :], 0), axis=1)
    source = slot // 64 * 8 + slot // 2 % 8
    arrived = lax.all_to_all(out, plane, 0, 0, tiled=True)
    arrived, *got = lax.optimization_barrier((arrived, *got))
    ordered = panel_order(source, slot // 16 % 4, slot % 2, arrived)
    final = lax.all_to_all(ordered, plane, 0, 0, tiled=True).reshape(32, 2, 4, 256)

    hosted = jnp.zeros((4, BLK, 2 * KV), BF)
    for k in (1, 2, 3):
        hosted = lax.dynamic_update_index_in_dim(hosted, got[k - 1], (y + 4 - k) % 4, 0)
    return final[:, 0].reshape(128, 256), final[:, 1].reshape(128, 256), hosted[None]


def solution(mesh):
    grid = Mesh(mesh.devices.reshape(4, 4, 4, 2), ("y", "x", "z", "c"))
    every, plane = ("y", "x", "z", "c"), ("x", "z", "c")
    placed = (
        P(every, None, None),
        P(every),
        P("y", None),
        P("y", None),
        P(),
        P("y", plane, None, None),
        P(every, None),
        P(every),
        P("y", plane, None, None),
    )
    return jax.shard_map(
        per_device,
        mesh=grid,
        in_specs=placed,
        out_specs=(P("y", plane), P("y", plane), P("y", plane, None, None)),
        check_vma=False,
    )
```

```python
import math

import jax
import jax.numpy as jnp
from jax import lax
from jax.experimental import pallas as pl
from jax.experimental.pallas import tpu as pltpu
from jax.sharding import Mesh
from jax.sharding import PartitionSpec as P

D = 8192
KVH = 8
HD = 128
PANELS = 128
BLK = 128
MAXB = 6
NBLK = 24
KV = KVH * HD
QKV = D + 2 * KV
GROUP = 1280
PR = 64
BF = jnp.bfloat16
F32 = jnp.float32
ROWS = 16
FIRST, LAST = (0, 2, 3, 4, 6, 7), (1, 2, 3, 5, 6, 7)
VMEM = 60 * 2**20


def shift(v, axis, k):
    return lax.ppermute(v, axis, [(i, (i + k) % 4) for i in range(4)])


def swap(v):
    return lax.ppermute(v, "c", [(0, 1), (1, 0)])


def split_kernel(place_ref, q_ref, k_ref, v_ref, *outs):
    step = pl.program_id(0)
    for out_ref, first, last in zip(outs, FIRST, LAST):

        @pl.when(jnp.logical_and(step >= first, step <= last))
        def _(out_ref=out_ref):
            for s in range(2):
                rows = slice(s * PR, (s + 1) * PR)
                out_ref[0, rows, :1024] = q_ref[s]
                out_ref[0, rows, 1024 : 1024 + HD] = k_ref[s]
                out_ref[0, rows, 1024 + HD :] = v_ref[s]


def split_heads(place, panels):
    def group(k, p):
        core = jnp.where(jnp.logical_or(k == 3, jnp.logical_or(k == 1, jnp.logical_or(k == 5, k == 7))), 1, 0)
        return lax.rem(p[0] + k // 2 + 1, 4) * 2 + lax.rem(p[1] + core, 2)

    def piece(first, last):
        return pl.BlockSpec(
            (1, 2 * PR, GROUP), lambda k, p: (jnp.clip(k, first, last) - first, 0, 0)
        )

    return pl.pallas_call(
        split_kernel,
        grid_spec=pltpu.PrefetchScalarGridSpec(
            num_scalar_prefetch=1,
            grid=(8,),
            in_specs=[
                pl.BlockSpec((2, PR, 1024), lambda k, p: (0, 0, group(k, p))),
                pl.BlockSpec((2, PR, HD), lambda k, p: (0, 0, D // HD + group(k, p))),
                pl.BlockSpec((2, PR, HD), lambda k, p: (0, 0, (D + KV) // HD + group(k, p))),
            ],
            out_specs=[piece(a, b) for a, b in zip(FIRST, LAST)],
        ),
        out_shape=[jax.ShapeDtypeStruct((n, 2 * PR, GROUP), BF) for n in (2, 1, 1, 2, 1, 1)],
        cost_estimate=pl.CostEstimate(flops=0, bytes_accessed=5_300_000, transcendentals=0),
        name="split_heads",
    )(place, panels, panels, panels)


def project_kernel(core_ref, *refs):
    rows, pieces, (out_ref, w_ref) = refs[:8], refs[8:16], refs[16:]
    core = core_ref[0]

    @pl.when(pl.program_id(0) == 0)
    def _():
        for i, piece in enumerate(pieces):
            slot = jnp.where(i % 2 == 0, core, 1 - core)
            at = pl.multiple_of((i // 2) * 256 + slot * 128, 128)
            w_ref[pl.ds(at, 128), :] = piece[0]

    mine = jnp.concatenate([r[...] for r in rows[:4]], axis=2)
    other = jnp.concatenate([r[...] for r in rows[4:]], axis=2)
    low = core == 0
    x = jnp.concatenate([jnp.where(low, mine, other), jnp.where(low, other, mine)], axis=1)
    x = x.reshape(256, 1024)
    for lo in range(0, GROUP, 256):
        total = jnp.dot(x, w_ref[:, lo : lo + 256], preferred_element_type=F32)
        out_ref[:, :, lo : lo + 256] = total.reshape(4, 64, 256).astype(BF)


def project(core, mine, other, *pieces):
    rows = pl.BlockSpec((4, 32, 256), lambda i, c: (i, 0, 0))
    return pl.pallas_call(
        project_kernel,
        grid_spec=pltpu.PrefetchScalarGridSpec(
            num_scalar_prefetch=1,
            grid=(4,),
            in_specs=[
                *[rows] * 8,
                *[pl.BlockSpec((1, 2 * PR, GROUP), lambda i, c, at=at: (at, 0, 0)) for _, at in pieces],
            ],
            out_specs=pl.BlockSpec((4, 64, GROUP), lambda i, c: (i, 0, 0)),
            scratch_shapes=[pltpu.VMEM((16 * PR, GROUP), BF)],
        ),
        out_shape=jax.ShapeDtypeStruct((16, 64, GROUP), BF),
        compiler_params=pltpu.CompilerParams(vmem_limit_bytes=VMEM),
        cost_estimate=pl.CostEstimate(flops=2_700_000_000, bytes_accessed=7_500_000, transcendentals=0),
        name="project",
    )(core, *mine, *other, *[v for v, _ in pieces])


def output_kernel(x_ref, *refs):
    pieces, (out_ref, sum_ref) = refs[:8], refs[8:]
    k = pl.program_id(0)

    @pl.when(k == 0)
    def _():
        sum_ref[...] = jnp.zeros_like(sum_ref)

    w = jnp.concatenate([r[0] for r in pieces], axis=0)
    sum_ref[...] += lax.dot_general(x_ref[...], w, (((1,), (1,)), ((), ())), preferred_element_type=F32)

    @pl.when(k == pl.num_programs(0) - 1)
    def _():
        out_ref[...] = sum_ref[...].reshape(32, 8, 512).astype(BF)


def output_product(x, w):
    return pl.pallas_call(
        output_kernel,
        grid=(4,),
        in_specs=[
            pl.BlockSpec((256, 2048), lambda k: (0, k)),
            *[pl.BlockSpec((1, PR, 2048), lambda k, i=i: (i, 0, k)) for i in range(8)],
        ],
        out_specs=pl.BlockSpec((32, 8, 512), lambda k: (0, 0, 0)),
        out_shape=jax.ShapeDtypeStruct((32, 8, 512), BF),
        scratch_shapes=[pltpu.VMEM((256, 512), F32)],
        compiler_params=pltpu.CompilerParams(vmem_limit_bytes=VMEM),
        cost_estimate=pl.CostEstimate(flops=2_150_000_000, bytes_accessed=12_800_000, transcendentals=0),
        name="output_product",
    )(x, *[w] * 8)


def pick_kernel(ids_ref, core_ref, first_ref, second_ref, scale_ref, gain_ref, out_ref):
    e = pl.program_id(0)
    lane = lax.broadcasted_iota(jnp.int32, (4, 32, 128), 2)
    scale = scale_ref[...]
    new = lax.broadcasted_iota(jnp.int32, (32, 32), 0)
    old = lax.broadcasted_iota(jnp.int32, (32, 32), 1)
    source = ((new // 4) % 2) * 16 + (new // 8) * 4 + new % 4
    turn = (old == source).astype(BF)

    def column(slot):
        p = ids_ref[e * 4 + slot]
        valid = p < PANELS
        p = jnp.where(valid, p, 0)
        at = pl.multiple_of((p // 2) * 128, 128)
        v = jnp.concatenate(
            [r[:, 0, :, pl.ds(at, 128)].astype(F32) for r in (first_ref, second_ref)], axis=1
        )
        v = v * scale * gain_ref[:, pl.ds(at, 128)].reshape(1, 1, 128)
        return jnp.where(valid, v, 0.0), p % 2

    for pair in range(2):
        a, odd_a = column(2 * pair)
        b, odd_b = column(2 * pair + 1)
        a = jnp.where(odd_a == 1, pltpu.roll(a, 64, 2), a)
        b = jnp.where(odd_b == 0, pltpu.roll(b, 64, 2), b)
        both = jnp.where(lane < 64, a, b).astype(BF)
        for x in range(4):
            turned = jnp.dot(turn, both[x], preferred_element_type=F32).astype(BF)
            out_ref[0, x, :, pair * 128 : (pair + 1) * 128] = turned


def pick_columns(ids, core, first, second, scale, gain):
    half = pl.BlockSpec((4, 1, 16, D), lambda e, ids, c: (0, c[0], 0, 0))
    return pl.pallas_call(
        pick_kernel,
        grid_spec=pltpu.PrefetchScalarGridSpec(
            num_scalar_prefetch=2,
            grid=(4,),
            in_specs=[
                half,
                half,
                pl.BlockSpec((4, 32, 1), lambda e, ids, c: (0, 0, 0)),
                pl.BlockSpec((1, D), lambda e, ids, c: (0, 0)),
            ],
            out_specs=pl.BlockSpec((1, 4, 32, 256), lambda e, ids, c: (e, 0, 0, 0)),
        ),
        out_shape=jax.ShapeDtypeStruct((4, 4, 32, 256), BF),
        compiler_params=pltpu.CompilerParams(vmem_limit_bytes=VMEM),
        cost_estimate=pl.CostEstimate(flops=20_000_000, bytes_accessed=3_000_000, transcendentals=0),
        name="pick_columns",
    )(ids, core, first, second, scale, gain)


def attend_kernel(table_ref, length_ref, q_ref, k_ref, v_ref, *refs):
    blocks, (out_ref, score_ref, prob_ref, sum_ref) = refs[:MAXB], refs[MAXB:]
    r = pl.program_id(0)
    length = length_ref[r]
    inverse_root = 1.0 / math.sqrt(HD)
    lane = lax.broadcasted_iota(jnp.int32, (16, 128), 1)
    row = lax.broadcasted_iota(jnp.int32, (16, 128), 0)
    fresh_seen = jnp.logical_or(lane == 0, jnp.logical_and(lane == 1, row >= 8))
    nt = (((1,), (1,)), ((), ()))
    pad = jnp.zeros((126, HD), F32)

    for b in range(MAXB):
        seen = b * BLK < length

        @pl.when(seen)
        def _(b=b):
            for g in range(KVH):
                keys = blocks[b][0, :, 2 * g * HD : (2 * g + 1) * HD]
                s = lax.dot_general(q_ref[0, g], keys, nt, preferred_element_type=F32) * inverse_root
                score_ref[b, g * 16 : (g + 1) * 16] = jnp.where(lane + b * BLK < length, s, -1e30)

        @pl.when(jnp.logical_not(seen))
        def _(b=b):
            score_ref[b] = jnp.full((128, 128), -1e30, F32)

    for g in range(KVH):
        new_k = jnp.concatenate([k_ref[0, :, g * HD : (g + 1) * HD].astype(F32), pad], axis=0)
        s = lax.dot_general(q_ref[0, g], new_k.astype(BF), nt, preferred_element_type=F32) * inverse_root
        score_ref[MAXB, g * 16 : (g + 1) * 16] = jnp.where(fresh_seen, s, -1e30)

    for g in range(KVH):
        rows = slice(g * 16, (g + 1) * 16)
        scores = [score_ref[b, rows] for b in range(MAXB + 1)]
        top = scores[0]
        for s in scores[1:]:
            top = jnp.maximum(top, s)
        top = jnp.max(top, axis=1, keepdims=True)
        weights = [jnp.exp(s - top) for s in scores]
        total = weights[0]
        for p in weights[1:]:
            total = total + p
        inverse = 1.0 / jnp.sum(total, axis=1, keepdims=True)
        for b in range(MAXB + 1):
            prob_ref[b, rows] = (weights[b] * inverse).astype(BF)

    for g in range(KVH):
        rows = slice(g * 16, (g + 1) * 16)
        new_v = jnp.concatenate([v_ref[0, :, g * HD : (g + 1) * HD].astype(F32), pad], axis=0)
        sum_ref[rows] = jnp.dot(prob_ref[MAXB, rows], new_v.astype(BF), preferred_element_type=F32)

    for b in range(MAXB):

        @pl.when(b * BLK < length)
        def _(b=b):
            for g in range(KVH):
                rows = slice(g * 16, (g + 1) * 16)
                vals = blocks[b][0, :, (2 * g + 1) * HD : (2 * g + 2) * HD]
                sum_ref[rows] += jnp.dot(prob_ref[b, rows], vals, preferred_element_type=F32)

    out_ref[0] = sum_ref[...].reshape(KVH, 16, HD).astype(BF)


def attend(table, length, q, k, v, cache):
    def block(b):
        return pl.BlockSpec((1, BLK, 2 * KV), lambda r, t, n: (t[r * MAXB + b], 0, 0))

    return pl.pallas_call(
        attend_kernel,
        grid_spec=pltpu.PrefetchScalarGridSpec(
            num_scalar_prefetch=2,
            grid=(4,),
            in_specs=[
                pl.BlockSpec((1, KVH, 16, HD), lambda r, t, n: (r, 0, 0, 0)),
                pl.BlockSpec((1, 2, KV), lambda r, t, n: (r, 0, 0)),
                pl.BlockSpec((1, 2, KV), lambda r, t, n: (r, 0, 0)),
                *[block(b) for b in range(MAXB)],
            ],
            out_specs=pl.BlockSpec((1, KVH, 16, HD), lambda r, t, n: (r, 0, 0, 0)),
            scratch_shapes=[
                pltpu.VMEM((MAXB + 1, 128, 128), F32),
                pltpu.VMEM((MAXB + 1, 128, 128), BF),
                pltpu.VMEM((128, HD), F32),
            ],
        ),
        out_shape=jax.ShapeDtypeStruct((4, KVH, 16, HD), BF),
        compiler_params=pltpu.CompilerParams(vmem_limit_bytes=VMEM),
        cost_estimate=pl.CostEstimate(flops=200_000_000, bytes_accessed=13_000_000, transcendentals=400_000),
        name="attend",
    )(table, length, q, k, v, *[cache] * MAXB)


def move_kernel(want_ref, table_ref, length_ref, fresh_ref, block_ref, out_ref):
    i = pl.program_id(0)
    b = want_ref[i]
    valid = b < NBLK
    out_ref[...] = jnp.where(valid, block_ref[...], jnp.zeros_like(block_ref))
    row = lax.broadcasted_iota(jnp.int32, (BLK, 2 * KV), 0)
    for r in range(4):
        for s in range(2):
            at = length_ref[r] + s
            hit = table_ref[r * MAXB + at // BLK] == b

            @pl.when(hit)
            def _(r=r, s=s, at=at):
                line = fresh_ref[2 * r + s : 2 * r + s + 1, :].astype(F32)
                old = out_ref[0].astype(F32)
                out_ref[0] = jnp.where(row == at % BLK, line, old).astype(BF)


def moved_blocks(want, table, length, fresh, cache):
    return pl.pallas_call(
        move_kernel,
        grid_spec=pltpu.PrefetchScalarGridSpec(
            num_scalar_prefetch=3,
            grid=(3,),
            in_specs=[
                pl.BlockSpec((8, 2 * KV), lambda i, w, t, n: (0, 0)),
                pl.BlockSpec((1, BLK, 2 * KV), lambda i, w, t, n: (jnp.minimum(w[i], NBLK - 1), 0, 0)),
            ],
            out_specs=pl.BlockSpec((1, BLK, 2 * KV), lambda i, w, t, n: (i, 0, 0)),
        ),
        out_shape=jax.ShapeDtypeStruct((3, BLK, 2 * KV), BF),
        compiler_params=pltpu.CompilerParams(vmem_limit_bytes=VMEM),
        cost_estimate=pl.CostEstimate(flops=1_000_000, bytes_accessed=3_200_000, transcendentals=0),
        name="moved_blocks",
    )(want, table, length, fresh, cache)


def order_kernel(from_ref, at_ref, half_ref, in_ref, out_ref):
    lane = lax.broadcasted_iota(jnp.int32, (8, 128), 1)

    def side(p, here):
        at = pl.multiple_of(at_ref[p] * 128, 128)
        v = in_ref[from_ref[p], :, pl.ds(at, 128)].astype(F32)
        return jnp.where(half_ref[p] == here, v, pltpu.roll(v, 64, 1))

    def step(q, _):
        for s in range(2):
            pair = 2 * q + s
            both = jnp.where(lane < 64, side(2 * pair, 0), side(2 * pair + 1, 1))
            out_ref[q, :, s * 128 : (s + 1) * 128] = both.astype(BF)
        return 0

    lax.fori_loop(0, 32, step, 0, unroll=4)


def panel_order(source, at, half, arrived):
    return pl.pallas_call(
        order_kernel,
        grid_spec=pltpu.PrefetchScalarGridSpec(
            num_scalar_prefetch=3,
            grid=(1,),
            in_specs=[pl.BlockSpec((32, 8, 512), lambda i, f, a, h: (0, 0, 0))],
            out_specs=pl.BlockSpec((32, 8, 256), lambda i, f, a, h: (0, 0, 0)),
        ),
        out_shape=jax.ShapeDtypeStruct((32, 8, 256), BF),
        name="panel_order",
    )(source, at, half, arrived)


def per_device(panels, panel_ids, first, second, gain, kv_cache, block_table, lengths, move_list):
    y, x = lax.axis_index("y"), lax.axis_index("x")
    z, c = lax.axis_index("z"), lax.axis_index("c")
    cache = kv_cache[0]
    table = block_table.reshape(-1)
    plane = ("x", "z", "c")

    right, far_a, far_b, left, own_a, own_b = split_heads(jnp.stack([z, c]), panels)
    panel_ids, right, left, far_a, far_b, w_o = lax.optimization_barrier(
        (panel_ids, right, left, far_a, far_b, panels[:, :, QKV:])
    )
    w_o = lax.all_gather(w_o, "y", axis=0, tiled=True)
    far_a = shift(far_a, "z", 1)
    far_b = shift(far_b, "z", -1)
    from_left = shift(right, "z", 1)
    from_right = shift(left, "z", -1)
    own_b = swap(own_b)

    near = lax.all_to_all(jnp.broadcast_to(panel_ids[None], (8, 2)), ("y", "c"), 0, 0, tiled=True)
    near = near.reshape(16)

    values = jnp.stack([first.reshape(4, 2, 16, D), second.reshape(4, 2, 16, D)]).astype(F32)
    scale = lax.rsqrt(jnp.mean(values * values, axis=-1) + 1e-06)
    scale = lax.dynamic_index_in_dim(scale, c, 2, keepdims=False)
    scale = scale.transpose(1, 0, 2).reshape(4, 32, 1)
    picked = pick_columns(
        near, c.reshape(1), first.reshape(4, 2, 16, D), second.reshape(4, 2, 16, D), scale, gain.reshape(1, D)
    )
    picked, far_a, far_b = lax.optimization_barrier((picked, far_a, far_b))
    far_a = shift(far_a, "z", 1)
    far_b = shift(far_b, "z", -1)
    rows = lax.all_to_all(picked, "y", 0, 0, tiled=True).reshape(16, 32, 256)
    rows_left = shift(rows, "z", 1)
    rows_right = shift(rows, "z", -1)
    rows_far = jnp.concatenate([shift(rows_left[:8], "z", 1), shift(rows_right[8:], "z", -1)], axis=0)
    mine = (rows, rows_right, rows_far, rows_left)
    other = tuple(swap(v) for v in mine)
    left_b = swap(from_left[1:])
    right_b = swap(from_right[1:])
    partial = project(
        c.reshape(1),
        mine,
        other,
        (own_a, 0),
        (own_b, 0),
        (from_right, 0),
        (right_b, 0),
        (far_a, 0),
        (swap(far_b), 0),
        (from_left, 0),
        (left_b, 0),
    )
    parts = lax.all_to_all(partial, ("y", "x"), 0, 0, tiled=True)
    parts, w_o = lax.optimization_barrier((parts, w_o))
    summed = jnp.sum(parts.astype(F32), axis=0).astype(BF)
    projected = lax.all_to_all(summed.reshape(8, 8, GROUP), ("z", "c"), 0, 0, tiled=True)
    projected = projected.reshape(KVH, 2, 4, GROUP)
    query = projected[..., :1024].reshape(KVH, 2, 4, 8, HD).transpose(2, 0, 1, 3, 4)
    query = query.reshape(4, KVH, 16, HD)
    fresh = projected[..., 1024:].transpose(2, 1, 0, 3)
    new_k = fresh[..., :HD].reshape(4, 2, KV)
    new_v = fresh[..., HD:].reshape(4, 2, KV)
    fresh = fresh.reshape(8, 2 * KV)

    want = move_list.reshape(4)
    want = jnp.stack([lax.dynamic_index_in_dim(want, (y + k) % 4, 0, keepdims=False) for k in (1, 2, 3)])
    moving = moved_blocks(want, table, lengths, fresh, cache)
    got = [shift(moving[k - 1], "y", k) for k in (1, 2, 3)]
    mixed = attend(table, lengths, query, new_k, new_v, cache)
    mixed = mixed.reshape(4, KVH, 2, 8, HD).transpose(2, 0, 1, 3, 4).reshape(8, D)
    mixed, near = lax.optimization_barrier((mixed, near))
    mixed = lax.all_gather(mixed, plane, axis=0, tiled=True)
    out = output_product(mixed, w_o)

    ids = lax.all_to_all(jnp.broadcast_to(near[None], (16, 16)), ("x", "z"), 0, 0, tiled=True)
    match = ids.reshape(1, 256) == jnp.arange(PANELS, dtype=jnp.int32)[:, None]
    slot = jnp.sum(jnp.where(match, jnp.arange(256, dtype=jnp.int32)[None, :], 0), axis=1)
    source = slot // 16 * 2 + slot // 2 % 2
    arrived = lax.all_to_all(out, plane, 0, 0, tiled=True)
    arrived, *got = lax.optimization_barrier((arrived, *got))
    ordered = panel_order(source, slot // 4 % 4, slot % 2, arrived)
    final = lax.all_to_all(ordered, plane, 0, 0, tiled=True).reshape(32, 2, 4, 256)

    hosted = jnp.zeros((4, BLK, 2 * KV), BF)
    for k in (1, 2, 3):
        hosted = lax.dynamic_update_index_in_dim(hosted, got[k - 1], (y + 4 - k) % 4, 0)
    return final[:, 0].reshape(128, 256), final[:, 1].reshape(128, 256), hosted[None]


def solution(mesh):
    grid = Mesh(mesh.devices.reshape(4, 4, 4, 2), ("y", "x", "z", "c"))
    every, plane = ("y", "x", "z", "c"), ("x", "z", "c")
    placed = (
        P(every, None, None),
        P(every),
        P("y", None),
        P("y", None),
        P(),
        P("y", plane, None, None),
        P(every, None),
        P(every),
        P("y", plane, None, None),
    )
    return jax.shard_map(
        per_device,
        mesh=grid,
        in_specs=placed,
        out_specs=(P("y", plane), P("y", plane), P("y", plane, None, None)),
        check_vma=False,
    )
```

```python
import math

import jax
import jax.numpy as jnp
from jax import lax
from jax.experimental import pallas as pl
from jax.experimental.pallas import tpu as pltpu
from jax.sharding import Mesh
from jax.sharding import PartitionSpec as P

D = 8192
KVH = 8
HD = 128
PANELS = 128
BLK = 128
MAXB = 6
NBLK = 24
KV = KVH * HD
QKV = D + 2 * KV
GROUP = 1280
PR = 64
BF = jnp.bfloat16
F32 = jnp.float32
ROWS = 16
FIRST, LAST = (0, 2, 3, 4, 6, 7), (1, 2, 3, 5, 6, 7)
VMEM = 60 * 2**20


def shift(v, axis, k):
    return lax.ppermute(v, axis, [(i, (i + k) % 4) for i in range(4)])


def swap(v):
    return lax.ppermute(v, "c", [(0, 1), (1, 0)])


def split_kernel(place_ref, q_ref, k_ref, v_ref, *outs):
    step = pl.program_id(0)
    for out_ref, first, last in zip(outs, FIRST, LAST):

        @pl.when(jnp.logical_and(step >= first, step <= last))
        def _(out_ref=out_ref):
            for s in range(2):
                rows = slice(s * PR, (s + 1) * PR)
                out_ref[0, rows, :1024] = q_ref[s]
                out_ref[0, rows, 1024 : 1024 + HD] = k_ref[s]
                out_ref[0, rows, 1024 + HD :] = v_ref[s]


def split_heads(place, panels):
    def group(k, p):
        core = jnp.where(jnp.logical_or(k == 3, jnp.logical_or(k == 1, jnp.logical_or(k == 5, k == 7))), 1, 0)
        return lax.rem(p[0] + k // 2 + 1, 4) * 2 + lax.rem(p[1] + core, 2)

    def piece(first, last):
        return pl.BlockSpec(
            (1, 2 * PR, GROUP), lambda k, p: (jnp.clip(k, first, last) - first, 0, 0)
        )

    return pl.pallas_call(
        split_kernel,
        grid_spec=pltpu.PrefetchScalarGridSpec(
            num_scalar_prefetch=1,
            grid=(8,),
            in_specs=[
                pl.BlockSpec((2, PR, 1024), lambda k, p: (0, 0, group(k, p))),
                pl.BlockSpec((2, PR, HD), lambda k, p: (0, 0, D // HD + group(k, p))),
                pl.BlockSpec((2, PR, HD), lambda k, p: (0, 0, (D + KV) // HD + group(k, p))),
            ],
            out_specs=[piece(a, b) for a, b in zip(FIRST, LAST)],
        ),
        out_shape=[jax.ShapeDtypeStruct((n, 2 * PR, GROUP), BF) for n in (2, 1, 1, 2, 1, 1)],
        cost_estimate=pl.CostEstimate(flops=0, bytes_accessed=5_300_000, transcendentals=0),
        name="split_heads",
    )(place, panels, panels, panels)


def project_kernel(core_ref, *refs):
    rows, pieces, (out_ref, w_ref) = refs[:8], refs[8:16], refs[16:]
    core = core_ref[0]

    @pl.when(pl.program_id(0) == 0)
    def _():
        for i, piece in enumerate(pieces):
            slot = jnp.where(i % 2 == 0, core, 1 - core)
            at = pl.multiple_of((i // 2) * 256 + slot * 128, 128)
            w_ref[pl.ds(at, 128), :] = piece[0]

    mine = jnp.concatenate([r[...] for r in rows[:4]], axis=2)
    other = jnp.concatenate([r[...] for r in rows[4:]], axis=2)
    low = core == 0
    x = jnp.concatenate([jnp.where(low, mine, other), jnp.where(low, other, mine)], axis=1)
    x = x.reshape(256, 1024)
    for lo in range(0, GROUP, 256):
        total = jnp.dot(x, w_ref[:, lo : lo + 256], preferred_element_type=F32)
        out_ref[:, :, lo : lo + 256] = total.reshape(4, 64, 256).astype(BF)


def project(core, mine, other, *pieces):
    rows = pl.BlockSpec((4, 32, 256), lambda i, c: (i, 0, 0))
    return pl.pallas_call(
        project_kernel,
        grid_spec=pltpu.PrefetchScalarGridSpec(
            num_scalar_prefetch=1,
            grid=(4,),
            in_specs=[
                *[rows] * 8,
                *[pl.BlockSpec((1, 2 * PR, GROUP), lambda i, c, at=at: (at, 0, 0)) for _, at in pieces],
            ],
            out_specs=pl.BlockSpec((4, 64, GROUP), lambda i, c: (i, 0, 0)),
            scratch_shapes=[pltpu.VMEM((16 * PR, GROUP), BF)],
        ),
        out_shape=jax.ShapeDtypeStruct((16, 64, GROUP), BF),
        compiler_params=pltpu.CompilerParams(vmem_limit_bytes=VMEM),
        cost_estimate=pl.CostEstimate(flops=2_700_000_000, bytes_accessed=7_500_000, transcendentals=0),
        name="project",
    )(core, *mine, *other, *[v for v, _ in pieces])


def output_kernel(x_ref, *refs):
    pieces, (out_ref, sum_ref) = refs[:8], refs[8:]
    k = pl.program_id(0)

    @pl.when(k == 0)
    def _():
        sum_ref[...] = jnp.zeros_like(sum_ref)

    w = jnp.concatenate([r[0] for r in pieces], axis=0)
    sum_ref[...] += lax.dot_general(x_ref[...], w, (((1,), (1,)), ((), ())), preferred_element_type=F32)

    @pl.when(k == pl.num_programs(0) - 1)
    def _():
        out_ref[...] = sum_ref[...].reshape(32, 8, 512).astype(BF)


def output_product(x, w):
    return pl.pallas_call(
        output_kernel,
        grid=(4,),
        in_specs=[
            pl.BlockSpec((256, 2048), lambda k: (0, k)),
            *[pl.BlockSpec((1, PR, 2048), lambda k, i=i: (i, 0, k)) for i in range(8)],
        ],
        out_specs=pl.BlockSpec((32, 8, 512), lambda k: (0, 0, 0)),
        out_shape=jax.ShapeDtypeStruct((32, 8, 512), BF),
        scratch_shapes=[pltpu.VMEM((256, 512), F32)],
        compiler_params=pltpu.CompilerParams(vmem_limit_bytes=VMEM),
        cost_estimate=pl.CostEstimate(flops=2_150_000_000, bytes_accessed=12_800_000, transcendentals=0),
        name="output_product",
    )(x, *[w] * 8)


def pick_kernel(ids_ref, core_ref, first_ref, second_ref, scale_ref, gain_ref, out_ref):
    e = pl.program_id(0)
    lane = lax.broadcasted_iota(jnp.int32, (4, 32, 128), 2)
    scale = scale_ref[...]
    new = lax.broadcasted_iota(jnp.int32, (32, 32), 0)
    old = lax.broadcasted_iota(jnp.int32, (32, 32), 1)
    source = ((new // 4) % 2) * 16 + (new // 8) * 4 + new % 4
    turn = (old == source).astype(BF)

    def column(slot):
        p = ids_ref[e * 4 + slot]
        valid = p < PANELS
        p = jnp.where(valid, p, 0)
        at = pl.multiple_of((p // 2) * 128, 128)
        v = jnp.concatenate(
            [r[:, 0, :, pl.ds(at, 128)].astype(F32) for r in (first_ref, second_ref)], axis=1
        )
        v = v * scale * gain_ref[:, pl.ds(at, 128)].reshape(1, 1, 128)
        return jnp.where(valid, v, 0.0), p % 2

    for pair in range(2):
        a, odd_a = column(2 * pair)
        b, odd_b = column(2 * pair + 1)
        a = jnp.where(odd_a == 1, pltpu.roll(a, 64, 2), a)
        b = jnp.where(odd_b == 0, pltpu.roll(b, 64, 2), b)
        both = jnp.where(lane < 64, a, b).astype(BF)
        for x in range(4):
            turned = jnp.dot(turn, both[x], preferred_element_type=F32).astype(BF)
            out_ref[0, x, :, pair * 128 : (pair + 1) * 128] = turned


def pick_columns(ids, core, first, second, scale, gain):
    half = pl.BlockSpec((4, 1, 16, D), lambda e, ids, c: (0, c[0], 0, 0))
    return pl.pallas_call(
        pick_kernel,
        grid_spec=pltpu.PrefetchScalarGridSpec(
            num_scalar_prefetch=2,
            grid=(4,),
            in_specs=[
                half,
                half,
                pl.BlockSpec((4, 32, 1), lambda e, ids, c: (0, 0, 0)),
                pl.BlockSpec((1, D), lambda e, ids, c: (0, 0)),
            ],
            out_specs=pl.BlockSpec((1, 4, 32, 256), lambda e, ids, c: (e, 0, 0, 0)),
        ),
        out_shape=jax.ShapeDtypeStruct((4, 4, 32, 256), BF),
        compiler_params=pltpu.CompilerParams(vmem_limit_bytes=VMEM),
        cost_estimate=pl.CostEstimate(flops=20_000_000, bytes_accessed=3_000_000, transcendentals=0),
        name="pick_columns",
    )(ids, core, first, second, scale, gain)


def attend_kernel(table_ref, length_ref, q_ref, k_ref, v_ref, *refs):
    blocks, (out_ref, score_ref, prob_ref, sum_ref) = refs[:MAXB], refs[MAXB:]
    r = pl.program_id(0)
    length = length_ref[r]
    inverse_root = 1.0 / math.sqrt(HD)
    lane = lax.broadcasted_iota(jnp.int32, (16, 128), 1)
    row = lax.broadcasted_iota(jnp.int32, (16, 128), 0)
    fresh_seen = jnp.logical_or(lane == 0, jnp.logical_and(lane == 1, row >= 8))
    nt = (((1,), (1,)), ((), ()))
    pad = jnp.zeros((126, HD), F32)

    for b in range(MAXB):
        seen = b * BLK < length

        @pl.when(seen)
        def _(b=b):
            for g in range(KVH):
                keys = blocks[b][0, :, 2 * g * HD : (2 * g + 1) * HD]
                s = lax.dot_general(q_ref[0, g], keys, nt, preferred_element_type=F32) * inverse_root
                score_ref[b, g * 16 : (g + 1) * 16] = jnp.where(lane + b * BLK < length, s, -1e30)

        @pl.when(jnp.logical_not(seen))
        def _(b=b):
            score_ref[b] = jnp.full((128, 128), -1e30, F32)

    for g in range(KVH):
        new_k = jnp.concatenate([k_ref[0, :, g * HD : (g + 1) * HD].astype(F32), pad], axis=0)
        s = lax.dot_general(q_ref[0, g], new_k.astype(BF), nt, preferred_element_type=F32) * inverse_root
        score_ref[MAXB, g * 16 : (g + 1) * 16] = jnp.where(fresh_seen, s, -1e30)

    for g in range(KVH):
        rows = slice(g * 16, (g + 1) * 16)
        scores = [score_ref[b, rows] for b in range(MAXB + 1)]
        top = scores[0]
        for s in scores[1:]:
            top = jnp.maximum(top, s)
        top = jnp.max(top, axis=1, keepdims=True)
        weights = [jnp.exp(s - top) for s in scores]
        total = weights[0]
        for p in weights[1:]:
            total = total + p
        inverse = 1.0 / jnp.sum(total, axis=1, keepdims=True)
        for b in range(MAXB + 1):
            prob_ref[b, rows] = (weights[b] * inverse).astype(BF)

    for g in range(KVH):
        rows = slice(g * 16, (g + 1) * 16)
        new_v = jnp.concatenate([v_ref[0, :, g * HD : (g + 1) * HD].astype(F32), pad], axis=0)
        sum_ref[rows] = jnp.dot(prob_ref[MAXB, rows], new_v.astype(BF), preferred_element_type=F32)

    for b in range(MAXB):

        @pl.when(b * BLK < length)
        def _(b=b):
            for g in range(KVH):
                rows = slice(g * 16, (g + 1) * 16)
                vals = blocks[b][0, :, (2 * g + 1) * HD : (2 * g + 2) * HD]
                sum_ref[rows] += jnp.dot(prob_ref[b, rows], vals, preferred_element_type=F32)

    out_ref[0] = sum_ref[...].reshape(KVH, 16, HD).astype(BF)


def attend(table, length, q, k, v, cache):
    def block(b):
        return pl.BlockSpec((1, BLK, 2 * KV), lambda r, t, n: (t[r * MAXB + b], 0, 0))

    return pl.pallas_call(
        attend_kernel,
        grid_spec=pltpu.PrefetchScalarGridSpec(
            num_scalar_prefetch=2,
            grid=(4,),
            in_specs=[
                pl.BlockSpec((1, KVH, 16, HD), lambda r, t, n: (r, 0, 0, 0)),
                pl.BlockSpec((1, 2, KV), lambda r, t, n: (r, 0, 0)),
                pl.BlockSpec((1, 2, KV), lambda r, t, n: (r, 0, 0)),
                *[block(b) for b in range(MAXB)],
            ],
            out_specs=pl.BlockSpec((1, KVH, 16, HD), lambda r, t, n: (r, 0, 0, 0)),
            scratch_shapes=[
                pltpu.VMEM((MAXB + 1, 128, 128), F32),
                pltpu.VMEM((MAXB + 1, 128, 128), BF),
                pltpu.VMEM((128, HD), F32),
            ],
        ),
        out_shape=jax.ShapeDtypeStruct((4, KVH, 16, HD), BF),
        compiler_params=pltpu.CompilerParams(vmem_limit_bytes=VMEM),
        cost_estimate=pl.CostEstimate(flops=200_000_000, bytes_accessed=13_000_000, transcendentals=400_000),
        name="attend",
    )(table, length, q, k, v, *[cache] * MAXB)


def move_kernel(want_ref, table_ref, length_ref, fresh_ref, block_ref, out_ref):
    i = pl.program_id(0)
    b = want_ref[i]
    valid = b < NBLK
    out_ref[...] = jnp.where(valid, block_ref[...], jnp.zeros_like(block_ref))
    row = lax.broadcasted_iota(jnp.int32, (BLK, 2 * KV), 0)
    for r in range(4):
        for s in range(2):
            at = length_ref[r] + s
            hit = table_ref[r * MAXB + at // BLK] == b

            @pl.when(hit)
            def _(r=r, s=s, at=at):
                line = fresh_ref[2 * r + s : 2 * r + s + 1, :].astype(F32)
                old = out_ref[0].astype(F32)
                out_ref[0] = jnp.where(row == at % BLK, line, old).astype(BF)


def moved_blocks(want, table, length, fresh, cache):
    return pl.pallas_call(
        move_kernel,
        grid_spec=pltpu.PrefetchScalarGridSpec(
            num_scalar_prefetch=3,
            grid=(3,),
            in_specs=[
                pl.BlockSpec((8, 2 * KV), lambda i, w, t, n: (0, 0)),
                pl.BlockSpec((1, BLK, 2 * KV), lambda i, w, t, n: (jnp.minimum(w[i], NBLK - 1), 0, 0)),
            ],
            out_specs=pl.BlockSpec((1, BLK, 2 * KV), lambda i, w, t, n: (i, 0, 0)),
        ),
        out_shape=jax.ShapeDtypeStruct((3, BLK, 2 * KV), BF),
        compiler_params=pltpu.CompilerParams(vmem_limit_bytes=VMEM),
        cost_estimate=pl.CostEstimate(flops=1_000_000, bytes_accessed=3_200_000, transcendentals=0),
        name="moved_blocks",
    )(want, table, length, fresh, cache)


def order_kernel(from_ref, at_ref, half_ref, in_ref, out_ref):
    lane = lax.broadcasted_iota(jnp.int32, (8, 128), 1)

    def side(p, here):
        at = pl.multiple_of(at_ref[p] * 128, 128)
        v = in_ref[from_ref[p], :, pl.ds(at, 128)].astype(F32)
        return jnp.where(half_ref[p] == here, v, pltpu.roll(v, 64, 1))

    def step(q, _):
        for s in range(2):
            pair = 2 * q + s
            both = jnp.where(lane < 64, side(2 * pair, 0), side(2 * pair + 1, 1))
            out_ref[q, :, s * 128 : (s + 1) * 128] = both.astype(BF)
        return 0

    lax.fori_loop(0, 32, step, 0, unroll=4)


def panel_order(source, at, half, arrived):
    return pl.pallas_call(
        order_kernel,
        grid_spec=pltpu.PrefetchScalarGridSpec(
            num_scalar_prefetch=3,
            grid=(1,),
            in_specs=[pl.BlockSpec((32, 8, 512), lambda i, f, a, h: (0, 0, 0))],
            out_specs=pl.BlockSpec((32, 8, 256), lambda i, f, a, h: (0, 0, 0)),
        ),
        out_shape=jax.ShapeDtypeStruct((32, 8, 256), BF),
        name="panel_order",
    )(source, at, half, arrived)


def per_device(panels, panel_ids, first, second, gain, kv_cache, block_table, lengths, move_list):
    y, x = lax.axis_index("y"), lax.axis_index("x")
    z, c = lax.axis_index("z"), lax.axis_index("c")
    cache = kv_cache[0]
    table = block_table.reshape(-1)
    plane = ("x", "z", "c")

    right, far_a, far_b, left, own_a, own_b = split_heads(jnp.stack([z, c]), panels)
    panel_ids, right, left, far_a, far_b, w_o = lax.optimization_barrier(
        (panel_ids, right, left, far_a, far_b, panels[:, :, QKV:])
    )
    w_o = lax.all_gather(w_o, "y", axis=0, tiled=True)
    far_a = shift(far_a, "z", 1)
    far_b = shift(far_b, "z", -1)
    from_left = shift(right, "z", 1)
    from_right = shift(left, "z", -1)
    own_b = swap(own_b)

    near = lax.all_to_all(jnp.broadcast_to(panel_ids[None], (8, 2)), ("y", "c"), 0, 0, tiled=True)
    near = near.reshape(16)

    values = jnp.stack([first.reshape(4, 2, 16, D), second.reshape(4, 2, 16, D)]).astype(F32)
    scale = lax.rsqrt(jnp.mean(values * values, axis=-1) + 1e-06)
    scale = lax.dynamic_index_in_dim(scale, c, 2, keepdims=False)
    scale = scale.transpose(1, 0, 2).reshape(4, 32, 1)
    picked = pick_columns(
        near, c.reshape(1), first.reshape(4, 2, 16, D), second.reshape(4, 2, 16, D), scale, gain.reshape(1, D)
    )
    picked, far_a, far_b = lax.optimization_barrier((picked, far_a, far_b))
    far_a = shift(far_a, "z", 1)
    far_b = shift(far_b, "z", -1)
    rows = lax.all_to_all(picked, "y", 0, 0, tiled=True).reshape(16, 32, 256)
    rows_left = shift(rows, "z", 1)
    rows_right = shift(rows, "z", -1)
    rows_far = jnp.concatenate([shift(rows_left[:8], "z", 1), shift(rows_right[8:], "z", -1)], axis=0)
    mine = (rows, rows_right, rows_far, rows_left)
    other = tuple(swap(v) for v in mine)
    near_b = swap(jnp.concatenate([from_left[1:], from_right[1:]], axis=0))
    partial = project(
        c.reshape(1),
        mine,
        other,
        (own_a, 0),
        (own_b, 0),
        (from_right, 0),
        (near_b, 1),
        (far_a, 0),
        (swap(far_b), 0),
        (from_left, 0),
        (near_b, 0),
    )
    parts = lax.all_to_all(partial, ("y", "x"), 0, 0, tiled=True)
    summed = jnp.sum(parts.astype(F32), axis=0).astype(BF)
    projected = lax.all_to_all(summed.reshape(8, 8, GROUP), ("z", "c"), 0, 0, tiled=True)
    projected, w_o = lax.optimization_barrier((projected, w_o))
    projected = projected.reshape(KVH, 2, 4, GROUP)
    query = projected[..., :1024].reshape(KVH, 2, 4, 8, HD).transpose(2, 0, 1, 3, 4)
    query = query.reshape(4, KVH, 16, HD)
    fresh = projected[..., 1024:].transpose(2, 1, 0, 3)
    new_k = fresh[..., :HD].reshape(4, 2, KV)
    new_v = fresh[..., HD:].reshape(4, 2, KV)
    fresh = fresh.reshape(8, 2 * KV)

    want = move_list.reshape(4)
    want = jnp.stack([lax.dynamic_index_in_dim(want, (y + k) % 4, 0, keepdims=False) for k in (1, 2, 3)])
    moving = moved_blocks(want, table, lengths, fresh, cache)
    got = [shift(moving[k - 1], "y", k) for k in (1, 2, 3)]
    mixed = attend(table, lengths, query, new_k, new_v, cache)
    mixed = mixed.reshape(4, KVH, 2, 8, HD).transpose(2, 0, 1, 3, 4).reshape(8, D)
    mixed, near = lax.optimization_barrier((mixed, near))
    mixed = lax.all_gather(mixed, plane, axis=0, tiled=True)
    out = output_product(mixed, w_o)

    ids = lax.all_to_all(jnp.broadcast_to(near[None], (16, 16)), ("x", "z"), 0, 0, tiled=True)
    match = ids.reshape(1, 256) == jnp.arange(PANELS, dtype=jnp.int32)[:, None]
    slot = jnp.sum(jnp.where(match, jnp.arange(256, dtype=jnp.int32)[None, :], 0), axis=1)
    source = slot // 16 * 2 + slot // 2 % 2
    arrived = lax.all_to_all(out, plane, 0, 0, tiled=True)
    arrived, *got = lax.optimization_barrier((arrived, *got))
    ordered = panel_order(source, slot // 4 % 4, slot % 2, arrived)
    final = lax.all_to_all(ordered, plane, 0, 0, tiled=True).reshape(32, 2, 4, 256)

    hosted = jnp.zeros((4, BLK, 2 * KV), BF)
    for k in (1, 2, 3):
        hosted = lax.dynamic_update_index_in_dim(hosted, got[k - 1], (y + 4 - k) % 4, 0)
    return final[:, 0].reshape(128, 256), final[:, 1].reshape(128, 256), hosted[None]


def solution(mesh):
    grid = Mesh(mesh.devices.reshape(4, 4, 4, 2), ("y", "x", "z", "c"))
    every, plane = ("y", "x", "z", "c"), ("x", "z", "c")
    placed = (
        P(every, None, None),
        P(every),
        P("y", None),
        P("y", None),
        P(),
        P("y", plane, None, None),
        P(every, None),
        P(every),
        P("y", plane, None, None),
    )
    return jax.shard_map(
        per_device,
        mesh=grid,
        in_specs=placed,
        out_specs=(P("y", plane), P("y", plane), P("y", plane, None, None)),
        check_vma=False,
    )
```
